256 devices in a mesh: loop: 64 (over z, y_hi, x), rep: 4 (over y_lo, core).
Axes of the slice: x: 4, y: 4 (y_hi: 2, y_lo: 2; y = y_hi * 2 + y_lo), z: 8, core: 2. Of those that a mesh axis runs over, the one named last changes fastest.
Arguments:
- descriptors: bfloat16 [65536, 128], P('loop'), may hold values from -6 to 6
- ard_scales: float32 [128], replicated, may hold values from 0.079549514 to 0.35355338
- noise: float32 [65536], P('loop'), may hold values from 0.1 to 1
- probes: float32 [16, 65536], P(None, 'loop'), may hold values from -7 to 7, as said below
Outputs:
- solution: float32 [16, 65536], P(None, 'loop')
- residual: float32 [16, 65536], P(None, 'loop')
- direction: float32 [16, 65536], P(None, 'loop')
The draws below stay inside these ranges and needn't reach their ends.
Inputs may be any that keep to these rules, and one draw needn't show every extreme that they name: `probes`: entries of order one.
All inputs are finite; a program needn't handle non-finite values.
Results may differ from the reference program's by a relative error of at most 0.014.
Values may be sent and summed in bfloat16 or wider, within the bound.
A program may use at most 64 MiB of HBM per device.

```python
import math
import jax
import jax.numpy as jnp
from jax import lax

FEAT = 128
PROBES = 16
NPTS = 65536


def draw_probes(key, part):
    key = jax.random.fold_in(key, 7)
    position = jnp.arange(NPTS, dtype=jnp.float32) / max(NPTS - 1, 1)
    growth = jnp.sqrt(1.0 + 2.0 * position)
    base = jnp.clip(jax.random.normal(key, (PROBES, NPTS), jnp.float32), -4.0, 4.0)
    return (base * growth[None, :]).astype(jnp.float32)


def level_of(own_key, extent, cuts, smallest, high):
    loudness = 1.0
    for axis_at, shards_of in cuts:
        heights = jax.random.uniform(jax.random.fold_in(jax.random.fold_in(own_key, 6), axis_at), (shards_of,), jnp.float32, smallest / len(cuts), high / len(cuts))
        loudness = loudness * jnp.repeat(jnp.exp(heights), extent[axis_at] // shards_of).reshape((-1,) + (1,) * (len(extent) - 1 - axis_at))
    return loudness


def bell_draw(rng, dims, spread, most, cuts=(), held_as=jnp.bfloat16):
    entries = spread * jax.random.normal(rng, dims, jnp.float32)
    if cuts:
        entries = entries * level_of(rng, dims, cuts, -0.22, 0.18)
    return jnp.clip(entries, -most, most).astype(held_as)


def setup_inputs(seed: int = 0) -> dict:
    seeds = jax.random.split(jax.random.key(seed), 5)
    descriptors = bell_draw(seeds[0], (NPTS, FEAT), 1.0, 6.0, ((0, 64),))
    ard_scales = jnp.clip(jnp.exp(jax.random.uniform(seeds[1], (FEAT,), jnp.float32, math.log(0.079549514), math.log(0.35355338))), 0.079549514, 0.35355338)
    noise = jnp.clip(jnp.exp(math.log(1.0) - 2.3025851 * jax.random.uniform(seeds[2], (NPTS,), jnp.float32) ** level_of(seeds[2], (NPTS,), ((0, 64),), -0.2, 0.2)), 0.1, 1.0)
    probes = draw_probes(jax.random.fold_in(seeds[4], 71), 0)
    return {"descriptors": descriptors, "ard_scales": ard_scales, "noise": noise, "probes": probes}


def prepare(descriptors, ard_scales):
    values = descriptors.astype(jnp.float32)
    unit = values * lax.rsqrt(lax.optimization_barrier(jnp.mean(values * values, axis=1, keepdims=True)) + 1e-06)
    scaled = (unit * ard_scales[None, :]).astype(jnp.bfloat16)
    widened = scaled.astype(jnp.float32)
    sqnorm = lax.optimization_barrier(jnp.sum(widened * widened, axis=1))
    return (scaled, sqnorm)

def reference(descriptors, ard_scales, noise, probes):
    scaled, sqnorm = prepare(descriptors, ard_scales)
    widened = scaled.astype(jnp.float32)
    vector = lax.optimization_barrier(probes.astype(jnp.bfloat16)).astype(jnp.float32)
    total_points = descriptors.shape[0]
    width = math.gcd(total_points, 1024)
    starts = jnp.arange(total_points // width, dtype=jnp.int32) * width

    def one_block(begin):
        target = lax.dynamic_slice_in_dim(widened, begin, width, 0)
        target_norm = lax.dynamic_slice_in_dim(sqnorm, begin, width, 0)
        cross = jnp.dot(widened, target.T, preferred_element_type=jnp.float32)
        distance = jnp.maximum(sqnorm[:, None] + target_norm[None, :] - 2.0 * cross, 0.0)
        kernel = lax.optimization_barrier(jnp.exp(-0.5 * distance).astype(jnp.bfloat16)).astype(jnp.float32)
        return jnp.dot(vector, kernel, preferred_element_type=jnp.float32)
    blocks = lax.map(one_block, starts)
    product = jnp.transpose(blocks, (1, 0, 2)).reshape(probes.shape[0], total_points)
    image = product + noise[None, :] * probes
    norm_old = lax.optimization_barrier(jnp.sum(probes * probes, axis=1))
    curve = lax.optimization_barrier(jnp.sum(probes * image, axis=1))
    alpha = norm_old / curve
    solution = alpha[:, None] * probes
    residual = probes - alpha[:, None] * image
    norm_new = lax.optimization_barrier(jnp.sum(residual * residual, axis=1))
    direction = residual + (norm_new / norm_old)[:, None] * probes
    return (solution, residual, direction)
```

```python
import functools

import jax
import jax.numpy as jnp
from jax import lax
from jax.experimental import pallas as pl
from jax.experimental.pallas import tpu as pltpu
from jax.sharding import PartitionSpec as P

MESH = pl.DeviceIdType.MESH
F32 = jnp.float32
BF16 = jnp.bfloat16

FEAT = 128
AUG = 16
PROBES = 16
SHARD = 1024
HALF = 512
QUART = 256
DEEP = FEAT + AUG
PACK = FEAT + AUG + PROBES

GROUPS = (
    ((0, 0), (-1, 0), (1, 0), (0, 1)),
    ((-2, 0), (2, 0), (-1, 1), (1, 1)),
    ((-3, 0), (3, 0), (-2, 1), (2, 1)),
    ((4, 0), (-3, 1), (3, 1), (4, 1)),
)
PLACE = {piece: (g, i) for g, group in enumerate(GROUPS) for i, piece in enumerate(group)}
UP = {(0, 0): (-1, 0), (-1, 0): (-2, 0), (-2, 0): (-3, 0), (-3, 0): (4, 0), (-2, 1): (-3, 1)}
DOWN = {(0, 0): (1, 0), (1, 0): (2, 0), (2, 0): (3, 0), (2, 1): (3, 1), (3, 1): (4, 1)}
ACROSS = {(0, 0): (0, 1), (-1, 0): (-1, 1), (1, 0): (1, 1), (-2, 0): (-2, 1), (2, 0): (2, 1)}
TARGET_X = (0, 1, 3, 2)


def partners():
    found = set()
    for dz in range(1, 8):
        found.add((0, 0, 0, dz, 0))
    for dx in range(4):
        for flip in range(2):
            for dc in range(2):
                found.add((dx, flip, flip, 0, dc))
            found.add((dx, 0, flip, 0, 0))
    found.discard((0, 0, 0, 0, 0))
    return sorted(found)


def kernel(
    desc_ref, ard_ref, noise_ref, probes_ref, image_ref, scalars_ref,
    sbuf, tbuf, acc, reduced, stats, sums1, sums2,
    ring_send, core_send, t_send, r_send, i_send, s1_send, s2_send,
    ring_recv, core_recv, t_recv, r_recv, i_recv, s1_recv, s2_recv,
):
    loop = lax.axis_index("loop")
    rep = lax.axis_index("rep")
    z, yh, x = loop // 8, (loop // 4) % 2, loop % 4
    yl, c = rep // 2, rep % 2

    def device(dx=0, dh=0, dl=0, dz=0, dc=0):
        nz = (z + dz) % 8
        nh = (yh + dh) % 2
        nx = (x + dx) % 4
        nl = (yl + dl) % 2
        nc = (c + dc) % 2
        return (nz * 8 + nh * 4 + nx, nl * 2 + nc)

    barrier = pltpu.get_barrier_semaphore()
    greeted = partners()
    for offsets in greeted:
        pl.semaphore_signal(barrier, inc=1, device_id=device(*offsets), device_id_type=MESH)

    half_at = pl.multiple_of(c * HALF, HALF)
    share = (yl + yh) % 2
    source_at = pl.multiple_of(share * HALF + c * QUART, QUART)

    def prepare(rows):
        values = rows.astype(F32)
        mean = jnp.mean(values * values, axis=1, keepdims=True)
        unit = values * lax.rsqrt(mean + 1e-06)
        scaled = (unit * ard_ref[...]).astype(BF16)
        turned = scaled.astype(F32).T
        norm = -0.5 * jnp.sum(turned * turned, axis=0, keepdims=True)
        high = norm.astype(BF16).astype(F32)
        rest = norm - high
        mid = rest.astype(BF16).astype(F32)
        low = rest - mid
        return turned.astype(BF16), (high, mid, low)

    def extra(parts, first):
        count = parts[0].shape[1]
        row = lax.broadcasted_iota(jnp.int32, (AUG, count), 0)
        ones = 3 - first
        out = jnp.where((row >= ones) & (row < ones + 3), 1.0, 0.0)
        for n, part in enumerate(parts):
            out = jnp.where(row == first + n, part, out)
        return out.astype(BF16)

    def own(i):
        return pl.ds(pl.multiple_of(i * HALF + c * QUART, QUART), QUART)

    turned, parts = prepare(desc_ref[pl.ds(source_at, QUART), :])
    sbuf[0, 0:FEAT, own(0)] = turned
    sbuf[0, FEAT:DEEP, own(0)] = extra(parts, 0)
    sbuf[0, DEEP:PACK, own(0)] = probes_ref[:, pl.ds(source_at, QUART)].astype(BF16)
    turned, parts = prepare(desc_ref[pl.ds(half_at, HALF), :])
    tbuf[0, 0:FEAT, :] = turned
    tbuf[0, FEAT:DEEP, :] = extra(parts, 3)

    pl.semaphore_wait(barrier, len(greeted))

    started = {}

    def begin(key, make):
        make().start()
        started[key] = make

    def copy(src, dst, send, recv, to):
        return pltpu.make_async_remote_copy(
            src_ref=src, dst_ref=dst, send_sem=send, recv_sem=recv, device_id=to, device_id_type=MESH
        )

    def ring(src, dst, to):
        (g, i), (h, j) = PLACE[src], PLACE[dst]
        return copy(
            sbuf.at[g, :, own(i)], sbuf.at[h, :, own(j)], ring_send.at[h, j], ring_recv.at[h, j], to
        )

    def to_core(piece):
        g, i = PLACE[piece]
        return copy(
            sbuf.at[g, :, own(i)], sbuf.at[g, :, own(i)], core_send.at[g, i], core_recv.at[g, i], sibling
        )

    def from_core(piece):
        g, i = PLACE[piece]
        there = pl.ds(pl.multiple_of(i * HALF + (1 - c) * QUART, QUART), QUART)
        return copy(
            sbuf.at[g, :, there], sbuf.at[g, :, there], core_send.at[g, i], core_recv.at[g, i], sibling
        )

    ways = ((UP, device(dz=1)), (DOWN, device(dz=7)), (ACROSS, device(dh=1, dl=1)))
    sibling = device(dc=1)

    def forward(piece):
        for table, to in ways:
            if piece in table:
                begin(("ring", table[piece]), functools.partial(ring, piece, table[piece], to))
        begin(("core", piece), functools.partial(to_core, piece))

    def arrive(piece):
        ring(piece, piece, device(dz=1)).wait_recv()
        forward(piece)

    def target_copy(t):
        return copy(
            tbuf.at[0], tbuf.at[t], t_send.at[t], t_recv.at[t], device(dx=(4 - TARGET_X[t]) % 4)
        )

    forward((0, 0))
    for t in (1, 2, 3):
        begin(("t", t), functools.partial(target_copy, t))

    acc[...] = jnp.zeros_like(acc)

    def block(g, t):
        cross = lax.dot_general(
            sbuf[g, 0:DEEP, :], tbuf[t], (((0,), (0,)), ((), ())), preferred_element_type=F32
        )
        weights = jnp.exp(jnp.minimum(cross, 0.0)).astype(BF16)
        acc[t] += jnp.dot(sbuf[g, DEEP:PACK, :], weights, preferred_element_type=F32)

    for piece in GROUPS[0][1:]:
        arrive(piece)
    for piece in GROUPS[0]:
        from_core(piece).wait_recv()

    def body0(t, carry):
        for n in (1, 2, 3):
            @pl.when(t == n)
            def _(n=n):
                target_copy(n).wait_recv()
                if n == 3:
                    for piece in GROUPS[1]:
                        arrive(piece)
        block(0, t)
        return carry

    lax.fori_loop(0, 4, body0, 0)
    for piece in GROUPS[1]:
        from_core(piece).wait_recv()

    def body1(t, carry):
        @pl.when(t == 3)
        def _():
            for piece in GROUPS[2]:
                arrive(piece)
        block(1, t)
        return carry

    lax.fori_loop(0, 4, body1, 0)
    for piece in GROUPS[2]:
        from_core(piece).wait_recv()

    def body2(t, carry):
        @pl.when(t == 2)
        def _():
            for piece in ((3, 1), (4, 0), (-3, 1)):
                arrive(piece)
        @pl.when(t == 3)
        def _():
            arrive((4, 1))
        block(2, t)
        return carry

    lax.fori_loop(0, 4, body2, 0)
    for piece in GROUPS[3]:
        from_core(piece).wait_recv()

    mine = x * 2 + yl

    def reduce_copy(t, dl):
        dx = TARGET_X[t]
        return copy(
            acc.at[t], reduced.at[mine], r_send.at[t, dl], r_recv.at[mine], device(dx=dx, dl=dl)
        )

    def body3(n, carry):
        t = 3 - n
        block(3, t)
        for s in (3, 2, 1, 0):
            @pl.when(t == s)
            def _(s=s):
                for dl in (1, 0) if s else (1,):
                    begin(("r", s, dl), functools.partial(reduce_copy, s, dl))
        return carry

    lax.fori_loop(0, 4, body3, 0)
    reduced[mine] = acc[0]
    for t in (0, 1, 2, 3):
        for dl in (1, 0) if t else (1,):
            other = ((x + TARGET_X[t]) % 4) * 2 + (yl + dl) % 2
            copy(
                acc.at[t], reduced.at[other], r_send.at[t, dl], r_recv.at[other], device(dx=TARGET_X[t], dl=dl)
            ).wait_recv()

    total = reduced[0]
    for n in range(1, 8):
        total = total + reduced[n]
    rhs = probes_ref[:, pl.ds(half_at, HALF)]
    image = total + noise_ref[:, pl.ds(half_at, HALF)] * rhs
    norm = jnp.sum(rhs * rhs, axis=1, keepdims=True)
    curve = jnp.sum(rhs * image, axis=1, keepdims=True)
    square = jnp.sum(image * image, axis=1, keepdims=True)
    lane = lax.broadcasted_iota(jnp.int32, (PROBES, 128), 1)
    packed = jnp.where(lane == 0, norm, jnp.where(lane == 1, curve, square))
    here = x * 4 + yh * 2 + c
    sums1[here] = packed
    peers = [(dx, flip, dc) for dx in range(4) for flip in range(2) for dc in range(2)][1:]
    for n, (dx, flip, dc) in enumerate(peers):
        begin(("s1", n), functools.partial(
            copy, sums1.at[here], sums1.at[here], s1_send.at[n], s1_recv.at[here],
            device(dx=dx, dh=flip, dl=flip, dc=dc),
        ))
    image_ref[:, pl.ds(half_at, HALF)] = image
    span = pl.ds(half_at, HALF)
    other_span = pl.ds(pl.multiple_of((1 - c) * HALF, HALF), HALF)
    begin("image", functools.partial(
        copy, image_ref.at[:, span], image_ref.at[:, span], i_send.at[0], i_recv.at[0], device(dc=1)
    ))
    for n, (dx, flip, dc) in enumerate(peers):
        there = ((x + dx) % 4) * 4 + ((yh + flip) % 2) * 2 + (c + dc) % 2
        copy(
            sums1.at[there], sums1.at[there], s1_send.at[n], s1_recv.at[there],
            device(dx=dx, dh=flip, dl=flip, dc=dc),
        ).wait_recv()
    whole = sums1[0]
    for n in range(1, 16):
        whole = whole + sums1[n]
    sums2[z] = whole
    for dz in range(1, 8):
        begin(("s2", dz), functools.partial(
            copy, sums2.at[z], sums2.at[z], s2_send.at[dz - 1], s2_recv.at[z], device(dz=dz)
        ))
    for dz in range(1, 8):
        there = (z + dz) % 8
        copy(sums2.at[there], sums2.at[there], s2_send.at[dz - 1], s2_recv.at[there], device(dz=dz)).wait_recv()
    whole = sums2[0]
    for n in range(1, 8):
        whole = whole + sums2[n]
    norm, curve, square = whole[:, 0:1], whole[:, 1:2], whole[:, 2:3]
    alpha = norm / curve
    fresh = jnp.maximum(alpha * alpha * square - norm, 0.0)
    scalars_ref[...] = jnp.where(lane == 0, alpha, fresh / norm)
    copy(
        image_ref.at[:, other_span], image_ref.at[:, other_span], i_send.at[0], i_recv.at[0], device(dc=1)
    ).wait_recv()
    for make in started.values():
        make().wait_send()


def local(descriptors, ard_scales, noise, probes):
    dma = pltpu.SemaphoreType.DMA
    vmem = pl.BlockSpec(memory_space=pltpu.VMEM)
    image, scalars = pl.pallas_call(
        kernel,
        out_shape=(
            jax.ShapeDtypeStruct((PROBES, SHARD), F32),
            jax.ShapeDtypeStruct((PROBES, 128), F32),
        ),
        in_specs=[vmem] * 4,
        out_specs=(vmem, vmem),
        scratch_shapes=[
            pltpu.VMEM((4, PACK, 4 * HALF), BF16),
            pltpu.VMEM((4, DEEP, HALF), BF16),
            pltpu.VMEM((4, PROBES, HALF), F32),
            pltpu.VMEM((8, PROBES, HALF), F32),
            pltpu.VMEM((PROBES, 128), F32),
            pltpu.VMEM((16, PROBES, 128), F32),
            pltpu.VMEM((8, PROBES, 128), F32),
            dma((4, 4)), dma((4, 4)), dma((4,)), dma((4, 2)), dma((1,)), dma((15,)), dma((7,)),
            dma((4, 4)), dma((4, 4)), dma((4,)), dma((8,)), dma((1,)), dma((16,)), dma((8,)),
        ],
        compiler_params=pltpu.CompilerParams(
            collective_id=0, has_side_effects=True, vmem_limit_bytes=56 << 20
        ),
        cost_estimate=pl.CostEstimate(flops=5_000_000_000, bytes_accessed=1_000_000, transcendentals=17_000_000),
        name="cg_step",
    )(descriptors, ard_scales.reshape(1, FEAT), noise.reshape(1, SHARD), probes)
    alpha, beta = scalars[:, 0:1], scalars[:, 1:2]
    residual = probes - alpha * image
    return alpha * probes, residual, residual + beta * probes


def solution(mesh):
    return jax.shard_map(
        local,
        mesh=mesh,
        in_specs=(P("loop", None), P(), P("loop"), P(None, "loop")),
        out_specs=(P(None, "loop"), P(None, "loop"), P(None, "loop")),
        check_vma=False,
    )
```

```python
import functools

import jax
import jax.numpy as jnp
from jax import lax
from jax.experimental import pallas as pl
from jax.experimental.pallas import tpu as pltpu
from jax.sharding import PartitionSpec as P

MESH = pl.DeviceIdType.MESH
F32 = jnp.float32
BF16 = jnp.bfloat16

FEAT = 128
AUG = 16
PROBES = 16
SHARD = 1024
HALF = 512
QUART = 256
DEEP = FEAT + AUG
PACK = FEAT + AUG + PROBES

PAIRS = (
    ((0, 0), (0, 1)),
    ((-1, 0), (1, 0)),
    ((-2, 0), (2, 0)),
    ((-1, 1), (1, 1)),
    ((-3, 0), (3, 0)),
    ((-2, 1), (2, 1)),
    ((4, 0), (-3, 1)),
    ((3, 1), (4, 1)),
)
PLACE = {piece: (g, i) for g, pair in enumerate(PAIRS) for i, piece in enumerate(pair)}
UP = {(0, 0): (-1, 0), (-1, 0): (-2, 0), (-2, 0): (-3, 0), (-3, 0): (4, 0), (-2, 1): (-3, 1)}
DOWN = {(0, 0): (1, 0), (1, 0): (2, 0), (2, 0): (3, 0), (2, 1): (3, 1), (3, 1): (4, 1)}
ACROSS = {(0, 0): (0, 1), (-1, 0): (-1, 1), (1, 0): (1, 1), (-2, 0): (-2, 1), (2, 0): (2, 1)}
TARGET_X = (0, 1, 3, 2)
NEAR = (
    (0, 0, 0, 1, 0), (0, 0, 0, 7, 0), (0, 1, 1, 0, 0), (0, 0, 0, 0, 1), (0, 0, 1, 0, 0),
    (1, 0, 0, 0, 0), (3, 0, 0, 0, 0), (2, 0, 0, 0, 0),
)
PEERS = sorted(
    ((dx, dy, dz) for dx in range(4) for dy in range(2) for dz in range(8) if dx or dy or dz),
    key=lambda o: -(min(o[0], 4 - o[0]) + o[1] + min(o[2], 8 - o[2])),
)


def kernel(
    desc_hbm, ard_hbm, noise_hbm, probes_hbm, solution_ref, residual_ref, direction_ref,
    desc_s, desc_t, ard_ref, noise_ref, probes_ref, sbuf, tbuf, acc, reduced, image_ref, rows, sums,
    in_sem, ring_send, core_send, t_send, r_send, i_send, row_send, sum_send,
    ring_recv, core_recv, t_recv, r_recv, i_recv, row_recv, sum_recv,
):
    loop = lax.axis_index("loop")
    rep = lax.axis_index("rep")
    z, yh, x = loop // 8, (loop // 4) % 2, loop % 4
    yl, c = rep // 2, rep % 2

    def device(dx=0, dh=0, dl=0, dz=0, dc=0):
        nz = (z + dz) % 8
        nh = (yh + dh) % 2
        nx = (x + dx) % 4
        nl = (yl + dl) % 2
        nc = (c + dc) % 2
        return (nz * 8 + nh * 4 + nx, nl * 2 + nc)

    barrier = pltpu.get_barrier_semaphore()
    for offsets in NEAR:
        pl.semaphore_signal(barrier, inc=1, device_id=device(*offsets), device_id_type=MESH)

    half_at = pl.multiple_of(c * HALF, HALF)
    share = (yl + yh) % 2
    source_at = pl.multiple_of(share * HALF + c * QUART, QUART)

    fetches = [
        pltpu.make_async_copy(src, dst, in_sem.at[n])
        for n, (src, dst) in enumerate((
            (desc_hbm.at[pl.ds(source_at, QUART)], desc_s),
            (ard_hbm, ard_ref),
            (probes_hbm, probes_ref),
            (desc_hbm.at[pl.ds(half_at, HALF)], desc_t),
            (noise_hbm, noise_ref),
        ))
    ]
    for fetch in fetches:
        fetch.start()

    def prepare(points):
        values = points.astype(F32)
        mean = jnp.mean(values * values, axis=1, keepdims=True)
        unit = values * lax.rsqrt(mean + 1e-06)
        scaled = (unit * ard_ref[...]).astype(BF16)
        turned = scaled.astype(F32).T
        norm = -0.5 * jnp.sum(turned * turned, axis=0, keepdims=True)
        high = norm.astype(BF16).astype(F32)
        rest = norm - high
        mid = rest.astype(BF16).astype(F32)
        low = rest - mid
        return turned.astype(BF16), (high, mid, low)

    def extra(parts, first):
        count = parts[0].shape[1]
        row = lax.broadcasted_iota(jnp.int32, (AUG, count), 0)
        ones = 3 - first
        out = jnp.where((row >= ones) & (row < ones + 3), 1.0, 0.0)
        for n, part in enumerate(parts):
            out = jnp.where(row == first + n, part, out)
        return out.astype(BF16)

    def own(i):
        return pl.ds(pl.multiple_of(i * HALF + c * QUART, QUART), QUART)

    started = {}

    def begin(key, make):
        make().start()
        started[key] = make

    def copy(src, dst, send, recv, to):
        return pltpu.make_async_remote_copy(
            src_ref=src, dst_ref=dst, send_sem=send, recv_sem=recv, device_id=to, device_id_type=MESH
        )

    def ring(src, dst, to):
        (g, i), (h, j) = PLACE[src], PLACE[dst]
        return copy(
            sbuf.at[g, :, own(i)], sbuf.at[h, :, own(j)], ring_send.at[h, j], ring_recv.at[h, j], to
        )

    ways = ((UP, device(dz=1)), (DOWN, device(dz=7)), (ACROSS, device(dh=1, dl=1)))
    sibling = device(dc=1)

    def to_core(piece):
        g, i = PLACE[piece]
        return copy(
            sbuf.at[g, :, own(i)], sbuf.at[g, :, own(i)], core_send.at[g, i], core_recv.at[g, i], sibling
        )

    def from_core(pair):
        for i in range(2):
            there = pl.ds(pl.multiple_of(i * HALF + (1 - c) * QUART, QUART), QUART)
            copy(
                sbuf.at[pair, :, there], sbuf.at[pair, :, there], core_send.at[pair, i],
                core_recv.at[pair, i], sibling,
            ).wait_recv()

    def forward(piece):
        for table, to in ways:
            if piece in table:
                begin(("ring", table[piece]), functools.partial(ring, piece, table[piece], to))
        begin(("core", piece), functools.partial(to_core, piece))

    def arrive(*pieces):
        for piece in pieces:
            ring(piece, piece, ways[0][1]).wait_recv()
            forward(piece)

    def quarter(t):
        return tbuf.at[t // 2, :, pl.ds(t % 2 * HALF, HALF)]

    def target_copy(t):
        return copy(quarter(0), quarter(t), t_send.at[t], t_recv.at[t], device(dx=(4 - TARGET_X[t]) % 4))

    for n in (0, 1, 2):
        fetches[n].wait()
    turned, parts = prepare(desc_s[...])
    sbuf[0, 0:FEAT, own(0)] = turned
    sbuf[0, FEAT:DEEP, own(0)] = extra(parts, 0)
    sbuf[0, DEEP:PACK, own(0)] = probes_ref[:, pl.ds(source_at, QUART)].astype(BF16)
    pl.semaphore_wait(barrier, len(NEAR))
    forward((0, 0))
    fetches[3].wait()
    turned, parts = prepare(desc_t[...])
    tbuf[0, 0:FEAT, 0:HALF] = turned
    tbuf[0, FEAT:DEEP, 0:HALF] = extra(parts, 3)
    for t in (1, 2, 3):
        begin(("t", t), functools.partial(target_copy, t))
    fetches[4].wait()
    acc[...] = jnp.zeros_like(acc)

    def block(pairs, targets):
        whole = None
        for pair in pairs:
            cross = lax.dot_general(
                sbuf[pair, 0:DEEP, :], targets, (((0,), (0,)), ((), ())), preferred_element_type=F32
            )
            weights = jnp.exp(jnp.minimum(cross, 0.0)).astype(BF16)
            part = jnp.dot(sbuf[pair, DEEP:PACK, :], weights, preferred_element_type=F32)
            whole = part if whole is None else whole + part
        return whole

    def quarter_of(t):
        return tbuf[t // 2, :, pl.ds(pl.multiple_of(t % 2 * HALF, HALF), HALF)]

    def events(step, table):
        for at, action in table.items():
            pl.when(step == at)(action)

    arrive((-1, 0), (1, 0), (0, 1))
    from_core(0)
    from_core(1)

    def target_here(t):
        return lambda: target_copy(t).wait_recv()

    def last_target():
        arrive((-2, 0), (2, 0))
        target_copy(3).wait_recv()

    def first(t, carry):
        events(t, {1: target_here(1), 2: target_here(2), 3: last_target})
        acc[t] += block((0, 1), quarter_of(t))
        return carry

    lax.fori_loop(0, 4, first, 0)

    def at0():
        arrive((-1, 1), (1, 1))
        from_core(2)

    def at2():
        arrive((3, 0), (-3, 0))
        from_core(3)

    def at4():
        arrive((-2, 1))
        from_core(4)

    def at6():
        arrive((3, 1))
        from_core(5)

    def middle(n, carry):
        events(n, {
            0: at0,
            2: at2,
            3: lambda: arrive((2, 1)),
            4: at4,
            6: at6,
            7: lambda: arrive((4, 0), (-3, 1)),
            8: lambda: from_core(6),
            9: lambda: arrive((4, 1)),
        })
        h = n % 2
        part = block((2 + n // 2,), tbuf[h])
        acc[2 * h] += part[:, 0:HALF]
        acc[2 * h + 1] += part[:, HALF:]
        return carry

    lax.fori_loop(0, 10, middle, 0)
    from_core(7)

    mine = x * 2 + yl

    def reduce_copy(t, dl):
        return copy(
            acc.at[t], reduced.at[mine], r_send.at[t, dl], r_recv.at[mine], device(dx=TARGET_X[t], dl=dl)
        )

    def leave(t):
        def action():
            for dl in (1, 0) if t else (1,):
                begin(("r", t, dl), functools.partial(reduce_copy, t, dl))
        return action

    def last(n, carry):
        t = 3 - n
        acc[t] += block((7,), quarter_of(t))
        events(t, {s: leave(s) for s in (3, 2, 1, 0)})
        return carry

    lax.fori_loop(0, 4, last, 0)
    reduced[mine] = acc[0]
    rhs = probes_ref[:, pl.ds(half_at, HALF)]
    diagonal = noise_ref[:, pl.ds(half_at, HALF)] * rhs
    norm = jnp.sum(rhs * rhs, axis=1, keepdims=True)
    for t in (3, 2, 1, 0):
        for dl in (1, 0) if t else (1,):
            other = ((x + TARGET_X[t]) % 4) * 2 + (yl + dl) % 2
            copy(
                acc.at[t], reduced.at[other], r_send.at[t, dl], r_recv.at[other], device(dx=TARGET_X[t], dl=dl)
            ).wait_recv()

    total = reduced[0]
    for n in range(1, 8):
        total = total + reduced[n]
    image = total + diagonal
    curve = jnp.sum(rhs * image, axis=1, keepdims=True)
    square = jnp.sum(image * image, axis=1, keepdims=True)

    lane = lax.broadcasted_iota(jnp.int32, (PROBES, 128), 1)
    probe = lax.broadcasted_iota(jnp.int32, (PROBES, 128), 0)
    spread = jnp.zeros((PROBES, 128), F32)
    for n, column in enumerate((norm, curve, square)):
        spread = jnp.where(lane == probe + PROBES * n, column, spread)
    rows[pl.ds(c, 1), :] = jnp.sum(spread, axis=0, keepdims=True)

    def row_copy(at):
        return copy(rows.at[pl.ds(at, 1)], rows.at[pl.ds(at, 1)], row_send.at[0], row_recv.at[0], sibling)

    begin("row", functools.partial(row_copy, c))
    span = pl.ds(half_at, HALF)
    image_ref[:, span] = image

    def image_copy(at):
        return copy(image_ref.at[:, at], image_ref.at[:, at], i_send.at[0], i_recv.at[0], sibling)

    row_copy(1 - c).wait_recv()
    sums[pl.ds(loop, 1), :] = rows[0:1, :] + rows[1:2, :]
    for dx, dy, dz in PEERS:
        copy(
            sums.at[pl.ds(loop, 1)], sums.at[pl.ds(loop, 1)], sum_send.at[0], sum_recv.at[0],
            device(dx=dx, dh=dy, dl=dy, dz=dz),
        ).start()
    begin("image", functools.partial(image_copy, span))
    image_copy(pl.ds(pl.multiple_of((1 - c) * HALF, HALF), HALF)).wait_recv()
    for make in started.values():
        make().wait_send()

    others = copy(
        sums.at[pl.ds(0, len(PEERS))], sums.at[pl.ds(0, len(PEERS))], sum_send.at[0], sum_recv.at[0], sibling
    )
    others.wait_recv()
    summed = jnp.sum(sums[...], axis=0, keepdims=True)

    def column(n):
        return jnp.sum(jnp.where(lane == probe + PROBES * n, summed, 0.0), axis=1, keepdims=True)

    norm, curve, square = column(0), column(1), column(2)
    alpha = norm / curve
    beta = jnp.maximum(alpha * alpha * square - norm, 0.0) / norm
    rhs = probes_ref[...]
    residual = rhs - alpha * image_ref[...]
    solution_ref[...] = alpha * rhs
    residual_ref[...] = residual
    direction_ref[...] = residual + beta * rhs
    others.wait_send()


def local(descriptors, ard_scales, noise, probes):
    dma = pltpu.SemaphoreType.DMA
    shape = jax.ShapeDtypeStruct((PROBES, SHARD), F32)
    return pl.pallas_call(
        kernel,
        out_shape=(shape, shape, shape),
        in_specs=[pl.BlockSpec(memory_space=pl.ANY)] * 4,
        out_specs=(pl.BlockSpec(memory_space=pltpu.VMEM),) * 3,
        scratch_shapes=[
            pltpu.VMEM((QUART, FEAT), BF16),
            pltpu.VMEM((HALF, FEAT), BF16),
            pltpu.VMEM((1, FEAT), F32),
            pltpu.VMEM((1, SHARD), F32),
            pltpu.VMEM((PROBES, SHARD), F32),
            pltpu.VMEM((8, PACK, 2 * HALF), BF16),
            pltpu.VMEM((2, DEEP, 2 * HALF), BF16),
            pltpu.VMEM((4, PROBES, HALF), F32),
            pltpu.VMEM((8, PROBES, HALF), F32),
            pltpu.VMEM((PROBES, SHARD), F32),
            pltpu.VMEM((8, 128), F32),
            pltpu.VMEM((64, 128), F32),
            dma((5,)),
            dma((8, 2)), dma((8, 2)), dma((4,)), dma((4, 2)), dma((1,)), dma((1,)), dma((1,)),
            dma((8, 2)), dma((8, 2)), dma((4,)), dma((8,)), dma((1,)), dma((1,)), dma((1,)),
        ],
        compiler_params=pltpu.CompilerParams(
            collective_id=0, has_side_effects=True, vmem_limit_bytes=56 << 20
        ),
        cost_estimate=pl.CostEstimate(flops=5_000_000_000, bytes_accessed=1_000_000, transcendentals=17_000_000),
        name="cg_step",
    )(descriptors, ard_scales.reshape(1, FEAT), noise.reshape(1, SHARD), probes)


def solution(mesh):
    return jax.shard_map(
        local,
        mesh=mesh,
        in_specs=(P("loop", None), P(), P("loop"), P(None, "loop")),
        out_specs=(P(None, "loop"), P(None, "loop"), P(None, "loop")),
        check_vma=False,
    )
```

```python
import functools

import jax
import jax.numpy as jnp
from jax import lax
from jax.experimental import pallas as pl
from jax.experimental.pallas import tpu as pltpu
from jax.sharding import PartitionSpec as P

MESH = pl.DeviceIdType.MESH
F32 = jnp.float32
BF16 = jnp.bfloat16

FEAT = 128
AUG = 16
PROBES = 16
SHARD = 1024
HALF = 512
QUART = 256
DEEP = FEAT + AUG
PACK = FEAT + AUG + PROBES
PART = 128

PAIRS = (
    ((0, 0), (0, 1)),
    ((-1, 0), (1, 0)),
    ((-2, 0), (2, 0)),
    ((-1, 1), (1, 1)),
    ((-3, 0), (3, 0)),
    ((-2, 1), (2, 1)),
    ((4, 0), (3, 1)),
    ((-3, 1), (4, 1)),
)
SPLIT = 4
PLACE = {piece: (g, i) for g, pair in enumerate(PAIRS) for i, piece in enumerate(pair)}
UP = {(0, 0): (-1, 0), (-1, 0): (-2, 0), (-2, 0): (-3, 0), (-3, 0): (4, 0), (-2, 1): (-3, 1)}
DOWN = {(0, 0): (1, 0), (1, 0): (2, 0), (2, 0): (3, 0), (2, 1): (3, 1), (3, 1): (4, 1)}
ACROSS = {(0, 0): (0, 1), (-1, 0): (-1, 1), (1, 0): (1, 1), (-2, 0): (-2, 1), (2, 0): (2, 1)}
TARGET_X = (0, 1, 3, 2)
NEAR = (
    (0, 0, 0, 1, 0), (0, 0, 0, 7, 0), (0, 1, 1, 0, 0), (0, 0, 0, 0, 1), (0, 0, 1, 0, 0),
    (1, 0, 0, 0, 0), (3, 0, 0, 0, 0), (2, 0, 0, 0, 0),
)
PEERS = sorted(
    ((dx, dy, dz) for dx in range(4) for dy in range(2) for dz in range(8) if dx or dy or dz),
    key=lambda o: -(min(o[0], 4 - o[0]) + o[1] + min(o[2], 8 - o[2])),
)


def kernel(
    desc_hbm, ard_hbm, noise_hbm, probes_hbm, alpha_ref, image_ref, beta_ref,
    desc_s, desc_t, ard_ref, noise_ref, probes_ref, sbuf, tbuf, acc, parting, reduced, rows, sums,
    in_sem, ring_send, core_send, t_send, r_send, i_send, row_send, sum_send,
    ring_recv, core_recv, t_recv, r_recv, i_recv, row_recv, sum_recv,
):
    loop = lax.axis_index("loop")
    rep = lax.axis_index("rep")
    z, yh, x = loop // 8, (loop // 4) % 2, loop % 4
    yl, c = rep // 2, rep % 2

    def device(dx=0, dh=0, dl=0, dz=0, dc=0):
        nz = (z + dz) % 8
        nh = (yh + dh) % 2
        nx = (x + dx) % 4
        nl = (yl + dl) % 2
        nc = (c + dc) % 2
        return (nz * 8 + nh * 4 + nx, nl * 2 + nc)

    barrier = pltpu.get_barrier_semaphore()
    for offsets in NEAR:
        pl.semaphore_signal(barrier, inc=1, device_id=device(*offsets), device_id_type=MESH)

    half_at = pl.multiple_of(c * HALF, HALF)
    share = (yl + yh) % 2
    source_at = pl.multiple_of(share * HALF + c * QUART, QUART)

    fetches = [
        pltpu.make_async_copy(src, dst, in_sem.at[n])
        for n, (src, dst) in enumerate((
            (desc_hbm.at[pl.ds(source_at, QUART)], desc_s),
            (ard_hbm, ard_ref),
            (probes_hbm, probes_ref),
            (desc_hbm.at[pl.ds(half_at, HALF)], desc_t),
            (noise_hbm, noise_ref),
        ))
    ]
    for fetch in fetches:
        fetch.start()

    def prepare(points):
        values = points.astype(F32)
        mean = jnp.mean(values * values, axis=1, keepdims=True)
        unit = values * lax.rsqrt(mean + 1e-06)
        scaled = (unit * ard_ref[...]).astype(BF16)
        turned = scaled.astype(F32).T
        norm = -0.5 * jnp.sum(turned * turned, axis=0, keepdims=True)
        high = norm.astype(BF16).astype(F32)
        rest = norm - high
        mid = rest.astype(BF16).astype(F32)
        low = rest - mid
        return turned.astype(BF16), (high, mid, low)

    def extra(parts, first):
        count = parts[0].shape[1]
        row = lax.broadcasted_iota(jnp.int32, (AUG, count), 0)
        ones = 3 - first
        out = jnp.where((row >= ones) & (row < ones + 3), 1.0, 0.0)
        for n, part in enumerate(parts):
            out = jnp.where(row == first + n, part, out)
        return out.astype(BF16)

    def place(piece, core, part):
        g, i = PLACE[piece]
        points = pl.ds(pl.multiple_of(i * QUART + core * PART, PART), PART)
        return sbuf.at[g, :, :, points] if part is None else sbuf.at[g, part, :, points]

    def parts_of(piece):
        return (0, 1) if PLACE[piece][0] < SPLIT else (None,)

    started = {}

    def begin(key, make):
        make().start()
        started[key] = make

    def copy(src, dst, send, recv, to):
        return pltpu.make_async_remote_copy(
            src_ref=src, dst_ref=dst, send_sem=send, recv_sem=recv, device_id=to, device_id_type=MESH
        )

    def ring(src, dst, part, to):
        at = PLACE[dst] + (part or 0,)
        return copy(place(src, c, part), place(dst, c, part), ring_send.at[at], ring_recv.at[at], to)

    ways = ((UP, device(dz=1)), (DOWN, device(dz=7)), (ACROSS, device(dh=1, dl=1)))
    sibling = device(dc=1)

    def core_copy(piece, part, core):
        at = PLACE[piece] + (part or 0,)
        return copy(place(piece, core, part), place(piece, core, part), core_send.at[at], core_recv.at[at], sibling)

    def from_core(pair, part=None):
        for piece in PAIRS[pair]:
            for p in parts_of(piece):
                if part is None or p == part:
                    core_copy(piece, p, 1 - c).wait_recv()

    def forward(piece, part):
        for table, to in ways:
            if piece in table:
                onward = table[piece]
                for p in parts_of(onward) if part is None else (part,):
                    begin(("ring", onward, p), functools.partial(ring, piece, onward, p, to))
        begin(("core", piece, part), functools.partial(core_copy, piece, part, c))

    def arrive(piece, part=None):
        for p in parts_of(piece) if part is None else (part,):
            ring(piece, piece, p, ways[0][1]).wait_recv()
        if part is None and parts_of(piece) == (0, 1):
            for table, to in ways:
                if piece in table:
                    begin(("ring", table[piece], None), functools.partial(ring, piece, table[piece], None, to))
            for p in (0, 1):
                begin(("core", piece, p), functools.partial(core_copy, piece, p, c))
        else:
            forward(piece, part)

    def target(t, first=0, count=HALF):
        return tbuf.at[t // 2, :, pl.ds(t % 2 * HALF + first, count)]

    def target_copy(t):
        return copy(target(0), target(t), t_send.at[t], t_recv.at[t], device(dx=(4 - TARGET_X[t]) % 4))

    def target_relay(t):
        half = (t - 1) * QUART
        return copy(
            target(t, half, QUART), target(3, half, QUART), t_send.at[t + 2], t_recv.at[t + 2],
            device(dx=(4 - TARGET_X[t]) % 4),
        )

    for n in (0, 1, 2):
        fetches[n].wait()
    turned, parts = prepare(desc_s[...])
    norms = extra(parts, 0)
    vector = probes_ref[:, pl.ds(source_at, QUART)].astype(BF16)
    points = pl.ds(pl.multiple_of(c * PART, PART), PART)
    for part in (0, 1):
        span = slice(part * PART, (part + 1) * PART)
        sbuf[0, part, 0:FEAT, points] = turned[:, span]
        sbuf[0, part, FEAT:DEEP, points] = norms[:, span]
        sbuf[0, part, DEEP:PACK, points] = vector[:, span]
    fetches[3].wait()
    turned, parts = prepare(desc_t[...])
    tbuf[0, 0:FEAT, 0:HALF] = turned
    tbuf[0, FEAT:DEEP, 0:HALF] = extra(parts, 3)
    pl.semaphore_wait(barrier, len(NEAR))
    forward((0, 0), 0)
    for t in (1, 2):
        begin(("t", t), functools.partial(target_copy, t))
    forward((0, 0), 1)
    fetches[4].wait()
    acc[...] = jnp.zeros_like(acc)

    def block(sources, targets):
        cross = lax.dot_general(
            sources[0:DEEP], targets, (((0,), (0,)), ((), ())), preferred_element_type=F32
        )
        weights = jnp.exp(jnp.minimum(cross, 0.0)).astype(BF16)
        return jnp.dot(sources[DEEP:PACK], weights, preferred_element_type=F32)

    def pair_of(g):
        return jnp.concatenate([sbuf[g, 0], sbuf[g, 1]], axis=1)

    def quarter_of(t):
        return tbuf[t // 2, :, pl.ds(pl.multiple_of(t % 2 * HALF, HALF), HALF)]

    def events(step, table):
        for at, action in table.items():
            pl.when(step == at)(action)

    def part_here(part):
        def action():
            for piece in ((-1, 0), (1, 0), (0, 1)):
                arrive(piece, part)
            from_core(0, part)
            from_core(1, part)
        return action

    def begins(part, carry):
        events(part, {0: part_here(0), 1: part_here(1)})
        acc[0] += block(jnp.concatenate([sbuf[0, part], sbuf[1, part]], axis=1), tbuf[0, :, 0:HALF])
        return carry

    lax.fori_loop(0, 2, begins, 0)

    def target_here(t):
        def action():
            target_copy(t).wait_recv()
            begin(("t", t + 2), functools.partial(target_relay, t))
        return action

    def second():
        for piece in ((-2, 0), (2, 0)):
            arrive(piece)

    def first(m, carry):
        events(m, {0: target_here(1), 2: target_here(2), 3: second})
        t = 1 + m // 2
        acc[t] += block(pair_of(m % 2), quarter_of(t))
        return carry

    lax.fori_loop(0, 4, first, 0)

    def at0():
        from_core(2)

    def at1():
        arrive((-1, 1))
        arrive((1, 1))
        for t in (1, 2):
            target_relay(t).wait_recv()
        for g in (0, 1):
            acc[3] += block(pair_of(g), tbuf[1, :, HALF:])

    def at2():
        arrive((3, 0))
        arrive((-3, 0))
        arrive((2, 1))
        from_core(3)

    def at4():
        arrive((-2, 1))
        from_core(4)

    def at6():
        arrive((3, 1))
        from_core(5)

    def at9():
        arrive((-3, 1))
        arrive((4, 1))

    def middle(n, carry):
        events(n, {
            0: at0,
            1: at1,
            2: at2,
            4: at4,
            6: at6,
            7: lambda: arrive((4, 0)),
            8: lambda: from_core(6),
            9: at9,
        })
        h = n % 2
        part = block(pair_of(2 + n // 2), tbuf[h])
        acc[2 * h] += part[:, 0:HALF]
        acc[2 * h + 1] += part[:, HALF:]
        return carry

    lax.fori_loop(0, 10, middle, 0)
    from_core(7)

    mine = x * 2 + yl

    def reduce_copy(t, dl):
        return copy(
            parting.at[t], reduced.at[mine], r_send.at[t, dl], r_recv.at[mine], device(dx=TARGET_X[t], dl=dl)
        )

    def leave(t):
        def action():
            for dl in (1, 0) if t else (1,):
                begin(("r", t, dl), functools.partial(reduce_copy, t, dl))
        return action

    def last(n, carry):
        t = 3 - n
        parting[t] = (acc[t] + block(pair_of(7), quarter_of(t))).astype(BF16)
        events(t, {s: leave(s) for s in (3, 2, 1, 0)})
        return carry

    lax.fori_loop(0, 4, last, 0)
    reduced[mine] = parting[0]
    rhs = probes_ref[:, pl.ds(half_at, HALF)]
    diagonal = noise_ref[:, pl.ds(half_at, HALF)] * rhs
    norm = jnp.sum(rhs * rhs, axis=1, keepdims=True)
    for t in (3, 2, 1, 0):
        for dl in (1, 0) if t else (1,):
            other = ((x + TARGET_X[t]) % 4) * 2 + (yl + dl) % 2
            copy(
                parting.at[t], reduced.at[other], r_send.at[t, dl], r_recv.at[other], device(dx=TARGET_X[t], dl=dl)
            ).wait_recv()

    total = reduced[0].astype(F32)
    for n in range(1, 8):
        total = total + reduced[n].astype(F32)
    image = total + diagonal
    curve = jnp.sum(rhs * image, axis=1, keepdims=True)
    square = jnp.sum(image * image, axis=1, keepdims=True)

    lane = lax.broadcasted_iota(jnp.int32, (PROBES, 128), 1)
    probe = lax.broadcasted_iota(jnp.int32, (PROBES, 128), 0)
    spread = jnp.zeros((PROBES, 128), F32)
    for n, column in enumerate((norm, curve, square)):
        spread = jnp.where(lane == probe + PROBES * n, column, spread)
    rows[pl.ds(c, 1), :] = jnp.sum(spread, axis=0, keepdims=True)

    def row_copy(at):
        return copy(rows.at[pl.ds(at, 1)], rows.at[pl.ds(at, 1)], row_send.at[0], row_recv.at[0], sibling)

    begin("row", functools.partial(row_copy, c))
    span = pl.ds(half_at, HALF)
    image_ref[:, span] = image

    def image_copy(at):
        return copy(image_ref.at[:, at], image_ref.at[:, at], i_send.at[0], i_recv.at[0], sibling)

    row_copy(1 - c).wait_recv()
    sums[pl.ds(loop, 1), :] = rows[0:1, :] + rows[1:2, :]
    for dx, dy, dz in PEERS:
        copy(
            sums.at[pl.ds(loop, 1)], sums.at[pl.ds(loop, 1)], sum_send.at[0], sum_recv.at[0],
            device(dx=dx, dh=dy, dl=dy, dz=dz),
        ).start()
    begin("image", functools.partial(image_copy, span))
    image_copy(pl.ds(pl.multiple_of((1 - c) * HALF, HALF), HALF)).wait_recv()
    for make in started.values():
        make().wait_send()

    others = copy(
        sums.at[pl.ds(0, len(PEERS))], sums.at[pl.ds(0, len(PEERS))], sum_send.at[0], sum_recv.at[0], sibling
    )
    others.wait_recv()
    summed = jnp.sum(sums[...], axis=0, keepdims=True)

    def column(n):
        return jnp.sum(jnp.where(lane == probe + PROBES * n, summed, 0.0), axis=1, keepdims=True)

    norm, curve, square = column(0), column(1), column(2)
    alpha = norm / curve
    beta = jnp.maximum(alpha * alpha * square - norm, 0.0) / norm
    alpha_ref[...] = jnp.broadcast_to(alpha, (PROBES, SHARD))
    beta_ref[...] = jnp.broadcast_to(beta, (PROBES, SHARD))
    others.wait_send()


def local(descriptors, ard_scales, noise, probes):
    dma = pltpu.SemaphoreType.DMA
    shape = pltpu.VMEM((PROBES, SHARD), F32)
    alpha, image, beta = pl.pallas_call(
        kernel,
        out_shape=(shape, shape, shape),
        in_specs=[pl.BlockSpec(memory_space=pl.ANY)] * 4,
        out_specs=(pl.BlockSpec(memory_space=pltpu.VMEM),) * 3,
        scratch_shapes=[
            pltpu.VMEM((QUART, FEAT), BF16),
            pltpu.VMEM((HALF, FEAT), BF16),
            pltpu.VMEM((1, FEAT), F32),
            pltpu.VMEM((1, SHARD), F32),
            pltpu.VMEM((PROBES, SHARD), F32),
            pltpu.VMEM((8, 2, PACK, HALF), BF16),
            pltpu.VMEM((2, DEEP, 2 * HALF), BF16),
            pltpu.VMEM((4, PROBES, HALF), F32),
            pltpu.VMEM((4, PROBES, HALF), BF16),
            pltpu.VMEM((8, PROBES, HALF), BF16),
            pltpu.VMEM((8, 128), F32),
            pltpu.VMEM((64, 128), F32),
            dma((5,)),
            dma((8, 2, 2)), dma((8, 2, 2)), dma((5,)), dma((4, 2)), dma((1,)), dma((1,)), dma((1,)),
            dma((8, 2, 2)), dma((8, 2, 2)), dma((5,)), dma((8,)), dma((1,)), dma((1,)), dma((1,)),
        ],
        compiler_params=pltpu.CompilerParams(
            collective_id=0, has_side_effects=True, vmem_limit_bytes=56 << 20
        ),
        cost_estimate=pl.CostEstimate(flops=5_000_000_000, bytes_accessed=1_000_000, transcendentals=17_000_000),
        name="cg_step",
    )(descriptors, ard_scales.reshape(1, FEAT), noise.reshape(1, SHARD), probes)
    residual = probes - alpha * image
    return alpha * probes, residual, residual + beta * probes


def solution(mesh):
    return jax.shard_map(
        local,
        mesh=mesh,
        in_specs=(P("loop", None), P(), P("loop"), P(None, "loop")),
        out_specs=(P(None, "loop"), P(None, "loop"), P(None, "loop")),
        check_vma=False,
    )
```

```python
import functools

import jax
import jax.numpy as jnp
from jax import lax
from jax.experimental import pallas as pl
from jax.experimental.pallas import tpu as pltpu
from jax.sharding import PartitionSpec as P

MESH = pl.DeviceIdType.MESH
F32 = jnp.float32
BF16 = jnp.bfloat16

FEAT = 128
AUG = 16
PROBES = 16
SHARD = 1024
HALF = 512
QUART = 256
DEEP = FEAT + AUG
PACK = FEAT + AUG + PROBES
PART = 128

PAIRS = (
    ((0, 0), (0, 1)),
    ((-1, 0), (1, 0)),
    ((-2, 0), (2, 0)),
    ((-1, 1), (1, 1)),
    ((-3, 0), (3, 0)),
    ((2, 1), (4, 0)),
    ((-2, 1), (3, 1)),
    ((4, 1), (-3, 1)),
)
SPLIT = 4
PLACE = {piece: (g, i) for g, pair in enumerate(PAIRS) for i, piece in enumerate(pair)}
UP = {(0, 0): (-1, 0), (-1, 0): (-2, 0), (-2, 0): (-3, 0), (-2, 1): (-3, 1)}
DOWN = {(0, 0): (1, 0), (1, 0): (2, 0), (2, 0): (3, 0), (2, 1): (3, 1)}
ACROSS = {(0, 0): (0, 1), (-1, 0): (-1, 1), (1, 0): (1, 1), (-2, 0): (-2, 1), (2, 0): (2, 1), (4, 0): (4, 1)}
NEXT = ((-1, 0), (1, 0), (0, 1))
ARRIVE = {0: ((((-1, 0), (1, 0), (0, 1)), 0),), 1: ((((-1, 0), (1, 0), (0, 1)), 1),), 6: ((((-2, 0), (2, 0)), None),), 7: ((((-1, 1), (1, 1)), None),), 8: ((((2, 1), (4, 0)), None),), 9: ((((3, 0), (-3, 0)), None),), 10: ((((-2, 1),), None),), 13: ((((3, 1),), None),), 14: ((((4, 1),), None),), 15: ((((-3, 1),), None),)}
CORE = {0: ((0, 0), (1, 0)), 1: ((0, 1), (1, 1)), 6: ((2, None),), 8: ((3, None),), 10: ((4, None),), 12: ((5, None),), 14: ((6, None),), 16: ((7, None),)}
TARGET = {2: (1,), 4: (2,)}
FAR = 2
TARGET_X = (0, 1, 3, 2)
NEAR = (
    (0, 0, 0, 1, 0), (0, 0, 0, 7, 0), (0, 1, 1, 0, 0), (0, 0, 0, 0, 1), (0, 0, 1, 0, 0),
    (1, 0, 0, 0, 0), (3, 0, 0, 0, 0), (2, 0, 0, 0, 0),
)
PEERS = sorted(
    ((dx, dy, dz, dc) for dx in range(4) for dy in range(2) for dz in range(8) for dc in range(2) if dx or dy or dz or dc),
    key=lambda o: -(min(o[0], 4 - o[0]) + o[1] + min(o[2], 8 - o[2])),
)


def kernel(
    desc_hbm, ard_hbm, noise_hbm, probes_hbm, alpha_ref, image_ref, beta_ref,
    desc_s, desc_t, ard_ref, noise_ref, probes_ref, sbuf, tbuf, acc, parting, reduced, sums,
    in_sem, ring_send, core_send, t_send, r_send, i_send, sum_send,
    ring_recv, core_recv, t_recv, r_recv, i_recv, sum_recv, ready1, ready2,
):
    loop = lax.axis_index("loop")
    rep = lax.axis_index("rep")
    z, yh, x = loop // 8, (loop // 4) % 2, loop % 4
    yl, c = rep // 2, rep % 2

    def device(dx=0, dh=0, dl=0, dz=0, dc=0):
        nz = (z + dz) % 8
        nh = (yh + dh) % 2
        nx = (x + dx) % 4
        nl = (yl + dl) % 2
        nc = (c + dc) % 2
        return (nz * 8 + nh * 4 + nx, nl * 2 + nc)

    barrier = pltpu.get_barrier_semaphore()
    for offsets in NEAR:
        pl.semaphore_signal(barrier, inc=1, device_id=device(*offsets), device_id_type=MESH)

    half_at = pl.multiple_of(c * HALF, HALF)
    share = (yl + yh) % 2
    source_at = pl.multiple_of(share * HALF + c * QUART, QUART)

    fetches = [
        pltpu.make_async_copy(src, dst, in_sem.at[n])
        for n, (src, dst) in enumerate((
            (desc_hbm.at[pl.ds(source_at, QUART)], desc_s),
            (ard_hbm, ard_ref),
            (probes_hbm, probes_ref),
            (desc_hbm.at[pl.ds(half_at, HALF)], desc_t),
            (noise_hbm, noise_ref),
        ))
    ]
    for fetch in fetches:
        fetch.start()

    def prepare(points):
        values = points.astype(F32)
        mean = jnp.mean(values * values, axis=1, keepdims=True)
        unit = values * lax.rsqrt(mean + 1e-06)
        scaled = (unit * ard_ref[...]).astype(BF16)
        turned = scaled.astype(F32).T
        norm = -0.5 * jnp.sum(turned * turned, axis=0, keepdims=True)
        high = norm.astype(BF16).astype(F32)
        rest = norm - high
        mid = rest.astype(BF16).astype(F32)
        low = rest - mid
        return turned.astype(BF16), (high, mid, low)

    def extra(parts, first):
        count = parts[0].shape[1]
        row = lax.broadcasted_iota(jnp.int32, (AUG, count), 0)
        ones = 3 - first
        out = jnp.where((row >= ones) & (row < ones + 3), 1.0, 0.0)
        for n, part in enumerate(parts):
            out = jnp.where(row == first + n, part, out)
        return out.astype(BF16)

    def place(piece, core, part):
        g, i = PLACE[piece]
        points = pl.ds(pl.multiple_of(i * QUART + core * PART, PART), PART)
        return sbuf.at[g, :, :, points] if part is None else sbuf.at[g, part, :, points]

    def parts_of(piece):
        return (0, 1) if PLACE[piece][0] < SPLIT else (None,)

    started = {}

    def begin(key, make):
        make().start()
        started[key] = make

    def copy(src, dst, send, recv, to):
        return pltpu.make_async_remote_copy(
            src_ref=src, dst_ref=dst, send_sem=send, recv_sem=recv, device_id=to, device_id_type=MESH
        )

    def ring(src, dst, part, to):
        at = PLACE[dst] + (part or 0,)
        return copy(place(src, c, part), place(dst, c, part), ring_send.at[at], ring_recv.at[at], to)

    ways = ((UP, device(dz=1)), (DOWN, device(dz=7)), (ACROSS, device(dh=1, dl=1)))
    sibling, opposite = device(dc=1), device(dz=4)

    def core_copy(piece, part, core):
        at = PLACE[piece] + (part or 0,)
        return copy(place(piece, core, part), place(piece, core, part), core_send.at[at], core_recv.at[at], sibling)

    def from_core(pair, part=None):
        for piece in PAIRS[pair]:
            for p in parts_of(piece):
                if part is None or p == part:
                    core_copy(piece, p, 1 - c).wait_recv()

    def forward(piece, part):
        for table, to in ways:
            if piece in table:
                onward = table[piece]
                for p in parts_of(onward) if part is None else (part,):
                    begin(("ring", onward, p), functools.partial(ring, piece, onward, p, to))
        begin(("core", piece, part), functools.partial(core_copy, piece, part, c))

    def arrive(piece, part=None):
        for p in parts_of(piece) if part is None else (part,):
            ring(piece, piece, p, ways[0][1]).wait_recv()
        if part is None and parts_of(piece) == (0, 1):
            for table, to in ways:
                if piece in table:
                    begin(("ring", table[piece], None), functools.partial(ring, piece, table[piece], None, to))
            for p in (0, 1):
                begin(("core", piece, p), functools.partial(core_copy, piece, p, c))
        else:
            forward(piece, part)

    def target(t, first=0, count=HALF):
        return tbuf.at[t // 2, :, pl.ds(t % 2 * HALF + first, count)]

    def target_copy(t):
        return copy(target(0), target(t), t_send.at[t], t_recv.at[t], device(dx=(4 - TARGET_X[t]) % 4))

    def target_relay(t):
        half = (t - 1) * QUART
        return copy(
            target(t, half, QUART), target(3, half, QUART), t_send.at[t + 2], t_recv.at[t + 2],
            device(dx=(4 - TARGET_X[t]) % 4),
        )

    for n in (0, 1, 2):
        fetches[n].wait()
    turned, parts = prepare(desc_s[...])
    norms = extra(parts, 0)
    vector = probes_ref[:, pl.ds(source_at, QUART)].astype(BF16)
    points = pl.ds(pl.multiple_of(c * PART, PART), PART)
    for part in (0, 1):
        span = slice(part * PART, (part + 1) * PART)
        sbuf[0, part, 0:FEAT, points] = turned[:, span]
        sbuf[0, part, FEAT:DEEP, points] = norms[:, span]
        sbuf[0, part, DEEP:PACK, points] = vector[:, span]
    fetches[3].wait()
    turned, parts = prepare(desc_t[...])
    tbuf[0, 0:FEAT, 0:HALF] = turned
    tbuf[0, FEAT:DEEP, 0:HALF] = extra(parts, 3)
    pl.semaphore_wait(barrier, len(NEAR))
    for dz in (1, 7):
        pl.semaphore_signal(ready1, inc=1, device_id=device(dz=dz), device_id_type=MESH)
    forward((0, 0), 0)
    for t in (1, 2):
        begin(("t", t), functools.partial(target_copy, t))
    forward((0, 0), 1)
    fetches[4].wait()
    acc[...] = jnp.zeros_like(acc)
    pl.semaphore_wait(ready1, 2)
    for dz in (2, 6):
        pl.semaphore_signal(ready2, inc=1, device_id=device(dz=dz), device_id_type=MESH)

    def block(sources, targets):
        cross = lax.dot_general(
            sources[0:DEEP], targets, (((0,), (0,)), ((), ())), preferred_element_type=F32
        )
        weights = jnp.exp(jnp.minimum(cross, 0.0)).astype(BF16)
        return jnp.dot(sources[DEEP:PACK], weights, preferred_element_type=F32)

    def pair_of(g):
        return jnp.concatenate([sbuf[g, 0], sbuf[g, 1]], axis=1)

    def quarter_of(t):
        return tbuf[t // 2, :, pl.ds(t % 2 * HALF if isinstance(t, int) else pl.multiple_of(t % 2 * HALF, HALF), HALF)]

    def target_here(t):
        target_copy(t).wait_recv()
        begin(("t", t + 2), functools.partial(target_relay, t))

    def far():
        pl.semaphore_wait(ready2, 2)
        begin(("ring", (4, 0), None), functools.partial(ring, (0, 0), (4, 0), None, opposite))

    def at(step):
        def action():
            for pieces, part in ARRIVE.get(step, ()):
                for piece in pieces:
                    arrive(piece, part)
            for pair, part in CORE.get(step, ()):
                from_core(pair, part)
            for t in TARGET.get(step, ()):
                target_here(t)
            if step == FAR:
                far()
        return action

    def events(index, first, count):
        for n in range(count):
            if first + n in ARRIVE or first + n in CORE or first + n in TARGET or first + n == FAR:
                if isinstance(index, int):
                    if index == n:
                        at(first + n)()
                else:
                    pl.when(index == n)(at(first + n))

    def own_targets(part, carry):
        events(part, 0, 2)
        acc[0] += block(jnp.concatenate([sbuf[0, part], sbuf[1, part]], axis=1), tbuf[0, :, 0:HALF])
        return carry

    for n in range(2):
        own_targets(n, 0)

    def next_targets(m, carry):
        events(m, 2, 4)
        t = 1 + m // 2
        acc[t] += block(pair_of(m % 2), quarter_of(t))
        return carry

    for n in range(4):
        next_targets(n, 0)

    def middle(n, carry):
        events(n, 6, 10)

        def extra_block():
            for t in (1, 2):
                target_relay(t).wait_recv()
            for g in (0, 1):
                acc[3] += block(pair_of(g), tbuf[1, :, HALF:])

        if isinstance(n, int):
            if n == 1:
                extra_block()
        else:
            pl.when(n == 1)(extra_block)
        h = n % 2
        part = block(pair_of(2 + n // 2), tbuf[h])
        acc[2 * h] += part[:, 0:HALF]
        acc[2 * h + 1] += part[:, HALF:]
        return carry

    for n in range(10):
        middle(n, 0)
    at(16)()

    mine = x * 2 + yl

    def reduce_copy(t, dl):
        return copy(
            parting.at[t], reduced.at[mine], r_send.at[t, dl], r_recv.at[mine], device(dx=TARGET_X[t], dl=dl)
        )

    def leave(t):
        def action():
            for dl in (1, 0) if t else (1,):
                begin(("r", t, dl), functools.partial(reduce_copy, t, dl))
        return action

    def last(n, carry):
        t = 3 - n
        parting[t] = (acc[t] + block(pair_of(7), quarter_of(t))).astype(BF16)
        if isinstance(t, int):
            leave(t)()
        else:
            for s in (3, 2, 1, 0):
                pl.when(t == s)(leave(s))
        return carry

    for n in range(4):
        last(n, 0)
    reduced[mine] = parting[0]
    rhs = probes_ref[:, pl.ds(half_at, HALF)]
    diagonal = noise_ref[:, pl.ds(half_at, HALF)] * rhs
    norm = jnp.sum(rhs * rhs, axis=1, keepdims=True)
    for t in (3, 2, 1, 0):
        for dl in (1, 0) if t else (1,):
            other = ((x + TARGET_X[t]) % 4) * 2 + (yl + dl) % 2
            copy(
                parting.at[t], reduced.at[other], r_send.at[t, dl], r_recv.at[other], device(dx=TARGET_X[t], dl=dl)
            ).wait_recv()

    total = reduced[0].astype(F32)
    for n in range(1, 8):
        total = total + reduced[n].astype(F32)
    image = total + diagonal
    curve = jnp.sum(rhs * image, axis=1, keepdims=True)
    square = jnp.sum(image * image, axis=1, keepdims=True)

    lane = lax.broadcasted_iota(jnp.int32, (PROBES, 128), 1)
    probe = lax.broadcasted_iota(jnp.int32, (PROBES, 128), 0)
    spread = jnp.zeros((PROBES, 128), F32)
    for n, column in enumerate((norm, curve, square)):
        spread = jnp.where(lane == probe + PROBES * n, column, spread)
    here = pl.ds(loop * 2 + c, 1)
    sums[here, :] = jnp.sum(spread, axis=0, keepdims=True)
    for dx, dy, dz, dc in PEERS:
        copy(
            sums.at[here], sums.at[here], sum_send.at[0], sum_recv.at[0],
            device(dx=dx, dh=dy, dl=dy, dz=dz, dc=dc),
        ).start()
    span = pl.ds(half_at, HALF)
    image_ref[:, span] = image

    def image_copy(at):
        return copy(image_ref.at[:, at], image_ref.at[:, at], i_send.at[0], i_recv.at[0], sibling)

    begin("image", functools.partial(image_copy, span))
    image_copy(pl.ds(pl.multiple_of((1 - c) * HALF, HALF), HALF)).wait_recv()
    for make in started.values():
        make().wait_send()

    others = copy(
        sums.at[pl.ds(0, len(PEERS))], sums.at[pl.ds(0, len(PEERS))], sum_send.at[0], sum_recv.at[0], sibling
    )
    others.wait_recv()
    summed = jnp.sum(sums[...], axis=0, keepdims=True)

    def column(n):
        return jnp.sum(jnp.where(lane == probe + PROBES * n, summed, 0.0), axis=1, keepdims=True)

    norm, curve, square = column(0), column(1), column(2)
    alpha = norm / curve
    beta = jnp.maximum(alpha * alpha * square - norm, 0.0) / norm
    alpha_ref[...] = jnp.broadcast_to(alpha, (PROBES, SHARD))
    beta_ref[...] = jnp.broadcast_to(beta, (PROBES, SHARD))
    others.wait_send()


def local(descriptors, ard_scales, noise, probes):
    dma = pltpu.SemaphoreType.DMA
    shape = pltpu.VMEM((PROBES, SHARD), F32)
    alpha, image, beta = pl.pallas_call(
        kernel,
        out_shape=(shape, shape, shape),
        in_specs=[pl.BlockSpec(memory_space=pl.ANY)] * 4,
        out_specs=(pl.BlockSpec(memory_space=pltpu.VMEM),) * 3,
        scratch_shapes=[
            pltpu.VMEM((QUART, FEAT), BF16),
            pltpu.VMEM((HALF, FEAT), BF16),
            pltpu.VMEM((1, FEAT), F32),
            pltpu.VMEM((1, SHARD), F32),
            pltpu.VMEM((PROBES, SHARD), F32),
            pltpu.VMEM((8, 2, PACK, HALF), BF16),
            pltpu.VMEM((2, DEEP, 2 * HALF), BF16),
            pltpu.VMEM((4, PROBES, HALF), F32),
            pltpu.VMEM((4, PROBES, HALF), BF16),
            pltpu.VMEM((8, PROBES, HALF), BF16),
            pltpu.VMEM((128, 128), F32),
            dma((5,)),
            dma((8, 2, 2)), dma((8, 2, 2)), dma((5,)), dma((4, 2)), dma((1,)), dma((1,)),
            dma((8, 2, 2)), dma((8, 2, 2)), dma((5,)), dma((8,)), dma((1,)), dma((1,)),
            pltpu.SemaphoreType.REGULAR, pltpu.SemaphoreType.REGULAR,
        ],
        compiler_params=pltpu.CompilerParams(
            collective_id=0, has_side_effects=True, vmem_limit_bytes=56 << 20
        ),
        cost_estimate=pl.CostEstimate(flops=5_000_000_000, bytes_accessed=1_000_000, transcendentals=17_000_000),
        name="cg_step",
    )(descriptors, ard_scales.reshape(1, FEAT), noise.reshape(1, SHARD), probes)
    residual = probes - alpha * image
    return alpha * probes, residual, residual + beta * probes


def solution(mesh):
    return jax.shard_map(
        local,
        mesh=mesh,
        in_specs=(P("loop", None), P(), P("loop"), P(None, "loop")),
        out_specs=(P(None, "loop"), P(None, "loop"), P(None, "loop")),
        check_vma=False,
    )
```

```python
import functools

import jax
import jax.numpy as jnp
from jax import lax
from jax.experimental import pallas as pl
from jax.experimental.pallas import tpu as pltpu
from jax.sharding import PartitionSpec as P

MESH = pl.DeviceIdType.MESH
F32 = jnp.float32
BF16 = jnp.bfloat16

FEAT = 128
AUG = 16
PROBES = 16
SHARD = 1024
HALF = 512
QUART = 256
DEEP = FEAT + AUG
PACK = FEAT + AUG + PROBES
PART = 128

PAIRS = (
    ((0, 0), (0, 1)),
    ((-1, 0), (1, 0)),
    ((-2, 0), (2, 0)),
    ((-1, 1), (1, 1)),
    ((-3, 0), (3, 0)),
    ((2, 1), (4, 0)),
    ((-2, 1), (3, 1)),
    ((4, 1), (-3, 1)),
)
PLACE = {piece: (g, i) for g, pair in enumerate(PAIRS) for i, piece in enumerate(pair)}
UP = {(0, 0): (-1, 0), (-1, 0): (-2, 0), (-2, 0): (-3, 0), (-2, 1): (-3, 1)}
DOWN = {(0, 0): (1, 0), (1, 0): (2, 0), (2, 0): (3, 0), (2, 1): (3, 1)}
ACROSS = {(0, 0): (0, 1), (-1, 0): (-1, 1), (1, 0): (1, 1), (-2, 0): (-2, 1), (2, 0): (2, 1), (4, 0): (4, 1)}
NEXT = ((-1, 0), (1, 0), (0, 1))
ARRIVE = {0: ((((-1, 0), (1, 0), (0, 1)), 0),), 1: ((((-1, 0), (1, 0), (0, 1)), 1),), 4: ((((-2, 0), (2, 0)), 0),), 5: ((((-2, 0), (2, 0)), 1),), 6: ((((-1, 1), (1, 1)), 0),), 7: ((((-1, 1), (1, 1)), 1),), 8: ((((2, 1), (-2, 1)), 0), (((3, 0), (-3, 0)), 0)), 9: ((((2, 1), (-2, 1)), 1), (((3, 0), (-3, 0)), 1), (((4, 0),), None)), 11: ((((3, 1),), 0),), 12: ((((-3, 1),), 0), (((3, 1),), 1)), 13: ((((-3, 1),), 1),), 14: ((((4, 1),), None),)}
CORE = {0: ((0, 0), (1, 0)), 1: ((0, 1), (1, 1)), 6: ((2, None),), 8: ((3, None),), 10: ((4, None),), 12: ((5, None),), 14: ((6, None),), 16: ((7, None),)}
TARGET = {2: (1,), 4: (2,)}
FAR = 3
TARGET_X = (0, 1, 3, 2)
NEAR = (
    (0, 0, 0, 1, 0), (0, 0, 0, 7, 0), (0, 1, 1, 0, 0), (0, 0, 0, 0, 1), (0, 0, 1, 0, 0),
    (1, 0, 0, 0, 0), (3, 0, 0, 0, 0), (2, 0, 0, 0, 0),
)
PEERS = sorted(
    ((dx, dy, dz, dc) for dx in range(4) for dy in range(2) for dz in range(8) for dc in range(2) if dx or dy or dz or dc),
    key=lambda o: -(min(o[0], 4 - o[0]) + o[1] + min(o[2], 8 - o[2])),
)


def kernel(
    desc_hbm, ard_hbm, noise_hbm, probes_hbm, alpha_ref, image_ref, beta_ref,
    desc_s, desc_t, ard_ref, noise_ref, probes_ref, sbuf, tbuf, acc, parting, reduced, sums,
    in_sem, ring_send, core_send, t_send, r_send, i_send, sum_send,
    ring_recv, core_recv, t_recv, r_recv, i_recv, sum_recv, ready1, ready2,
):
    loop = lax.axis_index("loop")
    rep = lax.axis_index("rep")
    z, yh, x = loop // 8, (loop // 4) % 2, loop % 4
    yl, c = rep // 2, rep % 2

    def device(dx=0, dh=0, dl=0, dz=0, dc=0):
        nz = (z + dz) % 8
        nh = (yh + dh) % 2
        nx = (x + dx) % 4
        nl = (yl + dl) % 2
        nc = (c + dc) % 2
        return (nz * 8 + nh * 4 + nx, nl * 2 + nc)

    barrier = pltpu.get_barrier_semaphore()
    for offsets in NEAR:
        pl.semaphore_signal(barrier, inc=1, device_id=device(*offsets), device_id_type=MESH)

    half_at = pl.multiple_of(c * HALF, HALF)
    share = (yl + yh) % 2
    source_at = pl.multiple_of(share * HALF + c * QUART, QUART)

    fetches = [
        pltpu.make_async_copy(src, dst, in_sem.at[n])
        for n, (src, dst) in enumerate((
            (desc_hbm.at[pl.ds(source_at, QUART)], desc_s),
            (ard_hbm, ard_ref),
            (probes_hbm, probes_ref),
            (desc_hbm.at[pl.ds(half_at, HALF)], desc_t),
            (noise_hbm, noise_ref),
        ))
    ]
    for fetch in fetches:
        fetch.start()

    def prepare(points):
        values = points.astype(F32)
        mean = jnp.mean(values * values, axis=1, keepdims=True)
        unit = values * lax.rsqrt(mean + 1e-06)
        scaled = (unit * ard_ref[...]).astype(BF16)
        turned = scaled.astype(F32).T
        norm = -0.5 * jnp.sum(turned * turned, axis=0, keepdims=True)
        high = norm.astype(BF16).astype(F32)
        rest = norm - high
        mid = rest.astype(BF16).astype(F32)
        low = rest - mid
        return turned.astype(BF16), (high, mid, low)

    def extra(parts, first):
        count = parts[0].shape[1]
        row = lax.broadcasted_iota(jnp.int32, (AUG, count), 0)
        ones = 3 - first
        out = jnp.where((row >= ones) & (row < ones + 3), 1.0, 0.0)
        for n, part in enumerate(parts):
            out = jnp.where(row == first + n, part, out)
        return out.astype(BF16)

    def place(piece, core, part):
        g, i = PLACE[piece]
        return sbuf.at[g, part, :, pl.ds(pl.multiple_of(i * QUART + core * PART, PART), PART)]

    started = {}

    def begin(key, make):
        make().start()
        started[key] = make

    def copy(src, dst, send, recv, to):
        return pltpu.make_async_remote_copy(
            src_ref=src, dst_ref=dst, send_sem=send, recv_sem=recv, device_id=to, device_id_type=MESH
        )

    def ring(src, dst, part, to):
        at = PLACE[dst] + (part,)
        return copy(place(src, c, part), place(dst, c, part), ring_send.at[at], ring_recv.at[at], to)

    ways = ((UP, device(dz=1)), (DOWN, device(dz=7)), (ACROSS, device(dh=1, dl=1)))
    sibling, opposite = device(dc=1), device(dz=4)

    def core_copy(piece, part, core):
        at = PLACE[piece] + (part,)
        return copy(place(piece, core, part), place(piece, core, part), core_send.at[at], core_recv.at[at], sibling)

    def from_core(pair, part):
        for p in (0, 1) if part is None else (part,):
            for piece in PAIRS[pair]:
                core_copy(piece, p, 1 - c).wait_recv()

    def forward(piece, part):
        for table, to in ways:
            if piece in table:
                begin(("ring", table[piece], part), functools.partial(ring, piece, table[piece], part, to))
        begin(("core", piece, part), functools.partial(core_copy, piece, part, c))

    def arrive(piece, part):
        for p in (0, 1) if part is None else (part,):
            ring(piece, piece, p, ways[0][1]).wait_recv()
            forward(piece, p)

    def target(t, first=0, count=HALF):
        return tbuf.at[t // 2, :, pl.ds(t % 2 * HALF + first, count)]

    def target_copy(t):
        return copy(target(0), target(t), t_send.at[t], t_recv.at[t], device(dx=(4 - TARGET_X[t]) % 4))

    def target_relay(t):
        half = (t - 1) * QUART
        return copy(
            target(t, half, QUART), target(3, half, QUART), t_send.at[t + 2], t_recv.at[t + 2],
            device(dx=(4 - TARGET_X[t]) % 4),
        )

    for n in (0, 1, 2):
        fetches[n].wait()
    turned, parts = prepare(desc_s[...])
    norms = extra(parts, 0)
    vector = probes_ref[:, pl.ds(source_at, QUART)].astype(BF16)
    points = pl.ds(pl.multiple_of(c * PART, PART), PART)
    for part in (0, 1):
        span = slice(part * PART, (part + 1) * PART)
        sbuf[0, part, 0:FEAT, points] = turned[:, span]
        sbuf[0, part, FEAT:DEEP, points] = norms[:, span]
        sbuf[0, part, DEEP:PACK, points] = vector[:, span]
    fetches[3].wait()
    turned, parts = prepare(desc_t[...])
    tbuf[0, 0:FEAT, 0:HALF] = turned
    tbuf[0, FEAT:DEEP, 0:HALF] = extra(parts, 3)
    pl.semaphore_wait(barrier, len(NEAR))
    for dz in (1, 7):
        pl.semaphore_signal(ready1, inc=1, device_id=device(dz=dz), device_id_type=MESH)
    forward((0, 0), 0)
    for t in (1, 2):
        begin(("t", t), functools.partial(target_copy, t))
    forward((0, 0), 1)
    fetches[4].wait()
    acc[...] = jnp.zeros_like(acc)
    pl.semaphore_wait(ready1, 2)
    for dz in (2, 6):
        pl.semaphore_signal(ready2, inc=1, device_id=device(dz=dz), device_id_type=MESH)

    def block(sources, targets):
        cross = lax.dot_general(
            sources[0:DEEP], targets, (((0,), (0,)), ((), ())), preferred_element_type=F32
        )
        weights = jnp.exp(jnp.minimum(cross, 0.0)).astype(BF16)
        return jnp.dot(sources[DEEP:PACK], weights, preferred_element_type=F32)

    def pair_of(g):
        return jnp.concatenate([sbuf[g, 0], sbuf[g, 1]], axis=1)

    def quarter_of(t):
        return tbuf[t // 2, :, pl.ds(t % 2 * HALF if isinstance(t, int) else pl.multiple_of(t % 2 * HALF, HALF), HALF)]

    def target_here(t):
        target_copy(t).wait_recv()
        begin(("t", t + 2), functools.partial(target_relay, t))

    def far():
        pl.semaphore_wait(ready2, 2)
        for p in (0, 1):
            begin(("ring", (4, 0), p), functools.partial(ring, (0, 0), (4, 0), p, opposite))

    def at(step):
        def action():
            for pieces, part in ARRIVE.get(step, ()):
                for piece in pieces:
                    arrive(piece, part)
            for pair, part in CORE.get(step, ()):
                from_core(pair, part)
            for t in TARGET.get(step, ()):
                target_here(t)
            if step == FAR:
                far()
        return action

    def events(index, first, count):
        for n in range(count):
            if first + n in ARRIVE or first + n in CORE or first + n in TARGET or first + n == FAR:
                if isinstance(index, int):
                    if index == n:
                        at(first + n)()
                else:
                    pl.when(index == n)(at(first + n))

    def own_targets(part, carry):
        events(part, 0, 2)
        acc[0] += block(jnp.concatenate([sbuf[0, part], sbuf[1, part]], axis=1), tbuf[0, :, 0:HALF])
        return carry

    for n in range(2):
        own_targets(n, 0)

    def next_targets(m, carry):
        events(m, 2, 4)
        t = 1 + m // 2
        acc[t] += block(pair_of(m % 2), quarter_of(t))
        return carry

    for n in range(4):
        next_targets(n, 0)

    def middle(n, carry):
        events(n, 6, 10)

        def extra_block():
            for t in (1, 2):
                target_relay(t).wait_recv()
            for g in (0, 1):
                acc[3] += block(pair_of(g), tbuf[1, :, HALF:])
            at(17)()

        if isinstance(n, int):
            if n == 1:
                extra_block()
        else:
            pl.when(n == 1)(extra_block)
        h = n % 2
        part = block(pair_of(2 + n // 2), tbuf[h])
        acc[2 * h] += part[:, 0:HALF]
        acc[2 * h + 1] += part[:, HALF:]
        return carry

    for n in range(10):
        middle(n, 0)
    at(16)()

    mine = x * 2 + yl

    def reduce_copy(t, dl):
        return copy(
            parting.at[t], reduced.at[mine], r_send.at[t, dl], r_recv.at[mine], device(dx=TARGET_X[t], dl=dl)
        )

    def leave(t):
        def action():
            for dl in (1, 0) if t else (1,):
                begin(("r", t, dl), functools.partial(reduce_copy, t, dl))
        return action

    def last(n, carry):
        t = 3 - n
        parting[t] = (acc[t] + block(pair_of(7), quarter_of(t))).astype(BF16)
        if isinstance(t, int):
            leave(t)()
        else:
            for s in (3, 2, 1, 0):
                pl.when(t == s)(leave(s))
        return carry

    for n in range(4):
        last(n, 0)
    reduced[mine] = parting[0]
    rhs = probes_ref[:, pl.ds(half_at, HALF)]
    diagonal = noise_ref[:, pl.ds(half_at, HALF)] * rhs
    norm = jnp.sum(rhs * rhs, axis=1, keepdims=True)
    for t in (3, 2, 1, 0):
        for dl in (1, 0) if t else (1,):
            other = ((x + TARGET_X[t]) % 4) * 2 + (yl + dl) % 2
            copy(
                parting.at[t], reduced.at[other], r_send.at[t, dl], r_recv.at[other], device(dx=TARGET_X[t], dl=dl)
            ).wait_recv()

    total = reduced[0].astype(F32)
    for n in range(1, 8):
        total = total + reduced[n].astype(F32)
    image = total + diagonal
    curve = jnp.sum(rhs * image, axis=1, keepdims=True)
    square = jnp.sum(image * image, axis=1, keepdims=True)

    lane = lax.broadcasted_iota(jnp.int32, (PROBES, 128), 1)
    probe = lax.broadcasted_iota(jnp.int32, (PROBES, 128), 0)
    spread = jnp.zeros((PROBES, 128), F32)
    for n, column in enumerate((norm, curve, square)):
        spread = jnp.where(lane == probe + PROBES * n, column, spread)
    here = pl.ds(loop * 2 + c, 1)
    sums[here, :] = jnp.sum(spread, axis=0, keepdims=True)
    for dx, dy, dz, dc in PEERS:
        copy(
            sums.at[here], sums.at[here], sum_send.at[0], sum_recv.at[0],
            device(dx=dx, dh=dy, dl=dy, dz=dz, dc=dc),
        ).start()
    span = pl.ds(half_at, HALF)
    image_ref[:, span] = image

    def image_copy(at):
        return copy(image_ref.at[:, at], image_ref.at[:, at], i_send.at[0], i_recv.at[0], sibling)

    begin("image", functools.partial(image_copy, span))
    image_copy(pl.ds(pl.multiple_of((1 - c) * HALF, HALF), HALF)).wait_recv()
    for make in started.values():
        make().wait_send()

    others = copy(
        sums.at[pl.ds(0, len(PEERS))], sums.at[pl.ds(0, len(PEERS))], sum_send.at[0], sum_recv.at[0], sibling
    )
    others.wait_recv()
    summed = jnp.sum(sums[...], axis=0, keepdims=True)

    def column(n):
        return jnp.sum(jnp.where(lane == probe + PROBES * n, summed, 0.0), axis=1, keepdims=True)

    norm, curve, square = column(0), column(1), column(2)
    alpha = norm / curve
    beta = jnp.maximum(alpha * alpha * square - norm, 0.0) / norm
    alpha_ref[...] = jnp.broadcast_to(alpha, (PROBES, SHARD))
    beta_ref[...] = jnp.broadcast_to(beta, (PROBES, SHARD))
    others.wait_send()


def local(descriptors, ard_scales, noise, probes):
    dma = pltpu.SemaphoreType.DMA
    shape = pltpu.VMEM((PROBES, SHARD), F32)
    alpha, image, beta = pl.pallas_call(
        kernel,
        out_shape=(shape, shape, shape),
        in_specs=[pl.BlockSpec(memory_space=pl.ANY)] * 4,
        out_specs=(pl.BlockSpec(memory_space=pltpu.VMEM),) * 3,
        scratch_shapes=[
            pltpu.VMEM((QUART, FEAT), BF16),
            pltpu.VMEM((HALF, FEAT), BF16),
            pltpu.VMEM((1, FEAT), F32),
            pltpu.VMEM((1, SHARD), F32),
            pltpu.VMEM((PROBES, SHARD), F32),
            pltpu.VMEM((8, 2, PACK, HALF), BF16),
            pltpu.VMEM((2, DEEP, 2 * HALF), BF16),
            pltpu.VMEM((4, PROBES, HALF), F32),
            pltpu.VMEM((4, PROBES, HALF), BF16),
            pltpu.VMEM((8, PROBES, HALF), BF16),
            pltpu.VMEM((128, 128), F32),
            dma((5,)),
            dma((8, 2, 2)), dma((8, 2, 2)), dma((5,)), dma((4, 2)), dma((1,)), dma((1,)),
            dma((8, 2, 2)), dma((8, 2, 2)), dma((5,)), dma((8,)), dma((1,)), dma((1,)),
            pltpu.SemaphoreType.REGULAR, pltpu.SemaphoreType.REGULAR,
        ],
        compiler_params=pltpu.CompilerParams(
            collective_id=0, has_side_effects=True, vmem_limit_bytes=56 << 20
        ),
        cost_estimate=pl.CostEstimate(flops=5_000_000_000, bytes_accessed=1_000_000, transcendentals=17_000_000),
        name="cg_step",
    )(descriptors, ard_scales.reshape(1, FEAT), noise.reshape(1, SHARD), probes)
    residual = probes - alpha * image
    return alpha * probes, residual, residual + beta * probes


def solution(mesh):
    return jax.shard_map(
        local,
        mesh=mesh,
        in_specs=(P("loop", None), P(), P("loop"), P(None, "loop")),
        out_specs=(P(None, "loop"), P(None, "loop"), P(None, "loop")),
        check_vma=False,
    )
```

```python
import functools

import jax
import jax.numpy as jnp
from jax import lax
from jax.experimental import pallas as pl
from jax.experimental.pallas import tpu as pltpu
from jax.sharding import PartitionSpec as P

MESH = pl.DeviceIdType.MESH
F32 = jnp.float32
BF16 = jnp.bfloat16

FEAT = 128
AUG = 16
PROBES = 16
SHARD = 1024
HALF = 512
QUART = 256
DEEP = FEAT + AUG
PACK = FEAT + AUG + PROBES
PART = 128

PAIRS = (
    ((0, 0), (0, 1)),
    ((-1, 0), (1, 0)),
    ((-2, 0), (2, 0)),
    ((-1, 1), (1, 1)),
    ((-3, 0), (3, 0)),
    ((2, 1), (4, 0)),
    ((-2, 1), (3, 1)),
    ((4, 1), (-3, 1)),
)
PLACE = {piece: (g, i) for g, pair in enumerate(PAIRS) for i, piece in enumerate(pair)}
UP = {(0, 0): (-1, 0), (-1, 0): (-2, 0), (-2, 0): (-3, 0), (-2, 1): (-3, 1)}
DOWN = {(0, 0): (1, 0), (1, 0): (2, 0), (2, 0): (3, 0), (2, 1): (3, 1)}
ACROSS = {(0, 0): (0, 1), (-1, 0): (-1, 1), (1, 0): (1, 1), (-2, 0): (-2, 1), (2, 0): (2, 1), (4, 0): (4, 1)}
NEXT = ((-1, 0), (1, 0), (0, 1))
ARRIVE = {0: ((((-1, 0), (1, 0), (0, 1)), 0),), 1: ((((-1, 0), (1, 0), (0, 1)), 1),), 4: ((((-2, 0), (2, 0)), 0),), 5: ((((-2, 0), (2, 0)), 1),), 6: ((((-1, 1), (1, 1)), 0),), 7: ((((-1, 1), (1, 1)), 1),), 8: ((((2, 1), (-2, 1)), 0), (((3, 0), (-3, 0)), 0)), 9: ((((2, 1), (-2, 1)), 1), (((3, 0), (-3, 0)), 1), (((4, 0),), None)), 11: ((((3, 1),), 0),), 12: ((((-3, 1),), 0), (((3, 1),), 1)), 13: ((((-3, 1),), 1),), 14: ((((4, 1),), None),)}
CORE = {0: ((0, 0), (1, 0)), 1: ((0, 1), (1, 1)), 6: ((2, None),), 8: ((3, None),), 10: ((4, None),), 12: ((5, None),), 14: ((6, None),), 16: ((7, None),)}
TARGET = {2: (1,), 4: (2,)}
FAR = 3
TARGET_X = (0, 1, 3, 2)
NEAR = (
    (0, 0, 0, 1, 0), (0, 0, 0, 7, 0), (0, 1, 1, 0, 0), (0, 0, 0, 0, 1), (0, 0, 1, 0, 0),
    (1, 0, 0, 0, 0), (3, 0, 0, 0, 0), (2, 0, 0, 0, 0),
)
PEERS = sorted(
    ((dx, dy, dz, dc) for dx in range(4) for dy in range(2) for dz in range(8) for dc in range(2) if dx or dy or dz or dc),
    key=lambda o: -(min(o[0], 4 - o[0]) + o[1] + min(o[2], 8 - o[2])),
)


def kernel(
    desc_hbm, ard_hbm, noise_hbm, probes_hbm, alpha_ref, image_ref, beta_ref,
    desc_s, desc_t, ard_ref, noise_ref, probes_ref, sbuf, tbuf, acc, parting, reduced, sums,
    in_sem, ring_send, core_send, t_send, r_send, i_send, sum_send,
    ring_recv, core_recv, t_recv, r_recv, i_recv, sum_recv, ready1, ready2,
):
    loop = lax.axis_index("loop")
    rep = lax.axis_index("rep")
    z, yh, x = loop // 8, (loop // 4) % 2, loop % 4
    yl, c = rep // 2, rep % 2

    def device(dx=0, dh=0, dl=0, dz=0, dc=0):
        nz = (z + dz) % 8
        nh = (yh + dh) % 2
        nx = (x + dx) % 4
        nl = (yl + dl) % 2
        nc = (c + dc) % 2
        return (nz * 8 + nh * 4 + nx, nl * 2 + nc)

    barrier = pltpu.get_barrier_semaphore()
    for offsets in NEAR:
        pl.semaphore_signal(barrier, inc=1, device_id=device(*offsets), device_id_type=MESH)

    half_at = pl.multiple_of(c * HALF, HALF)
    share = (yl + yh) % 2
    source_at = pl.multiple_of(share * HALF + c * QUART, QUART)

    fetches = [
        pltpu.make_async_copy(src, dst, in_sem.at[n])
        for n, (src, dst) in enumerate((
            (desc_hbm.at[pl.ds(source_at, QUART)], desc_s),
            (ard_hbm, ard_ref),
            (probes_hbm, probes_ref),
            (desc_hbm.at[pl.ds(half_at, HALF)], desc_t),
            (noise_hbm, noise_ref),
        ))
    ]
    for fetch in fetches:
        fetch.start()

    def prepare(points):
        values = points.astype(F32)
        mean = jnp.mean(values * values, axis=1, keepdims=True)
        unit = values * lax.rsqrt(mean + 1e-06)
        scaled = (unit * ard_ref[...]).astype(BF16)
        turned = scaled.astype(F32).T
        norm = -0.5 * jnp.sum(turned * turned, axis=0, keepdims=True)
        high = norm.astype(BF16).astype(F32)
        rest = norm - high
        mid = rest.astype(BF16).astype(F32)
        low = rest - mid
        return turned.astype(BF16), (high, mid, low)

    def extra(parts, first):
        count = parts[0].shape[1]
        row = lax.broadcasted_iota(jnp.int32, (AUG, count), 0)
        ones = 3 - first
        out = jnp.where((row >= ones) & (row < ones + 3), 1.0, 0.0)
        for n, part in enumerate(parts):
            out = jnp.where(row == first + n, part, out)
        return out.astype(BF16)

    def place(piece, core, part):
        g, i = PLACE[piece]
        return sbuf.at[g, part, :, pl.ds(pl.multiple_of(i * QUART + core * PART, PART), PART)]

    started = {}

    def begin(key, make):
        make().start()
        started[key] = make

    def copy(src, dst, send, recv, to):
        return pltpu.make_async_remote_copy(
            src_ref=src, dst_ref=dst, send_sem=send, recv_sem=recv, device_id=to, device_id_type=MESH
        )

    def ring(src, dst, part, to):
        at = PLACE[dst] + (part,)
        return copy(place(src, c, part), place(dst, c, part), ring_send.at[at], ring_recv.at[at], to)

    ways = ((UP, device(dz=1)), (DOWN, device(dz=7)), (ACROSS, device(dh=1, dl=1)))
    sibling, opposite = device(dc=1), device(dz=4)

    def core_copy(piece, part, core):
        at = PLACE[piece] + (part,)
        return copy(place(piece, core, part), place(piece, core, part), core_send.at[at], core_recv.at[at], sibling)

    def from_core(pair, part):
        for p in (0, 1) if part is None else (part,):
            for piece in PAIRS[pair]:
                core_copy(piece, p, 1 - c).wait_recv()

    def forward(piece, part):
        for table, to in ways:
            if piece in table:
                begin(("ring", table[piece], part), functools.partial(ring, piece, table[piece], part, to))
        begin(("core", piece, part), functools.partial(core_copy, piece, part, c))

    def arrive(piece, part):
        for p in (0, 1) if part is None else (part,):
            ring(piece, piece, p, ways[0][1]).wait_recv()
            forward(piece, p)

    def target(t, first=0, count=HALF):
        return tbuf.at[t // 2, :, pl.ds(t % 2 * HALF + first, count)]

    def target_copy(t):
        return copy(target(0), target(t), t_send.at[t], t_recv.at[t], device(dx=(4 - TARGET_X[t]) % 4))

    def target_relay(t):
        half = (t - 1) * QUART
        return copy(
            target(t, half, QUART), target(3, half, QUART), t_send.at[t + 2], t_recv.at[t + 2],
            device(dx=(4 - TARGET_X[t]) % 4),
        )

    for n in (0, 1, 2):
        fetches[n].wait()
    turned, parts = prepare(desc_s[...])
    norms = extra(parts, 0)
    vector = probes_ref[:, pl.ds(source_at, QUART)].astype(BF16)
    points = pl.ds(pl.multiple_of(c * PART, PART), PART)
    for part in (0, 1):
        span = slice(part * PART, (part + 1) * PART)
        sbuf[0, part, 0:FEAT, points] = turned[:, span]
        sbuf[0, part, FEAT:DEEP, points] = norms[:, span]
        sbuf[0, part, DEEP:PACK, points] = vector[:, span]
    fetches[3].wait()
    turned, parts = prepare(desc_t[...])
    tbuf[0, 0:FEAT, 0:HALF] = turned
    tbuf[0, FEAT:DEEP, 0:HALF] = extra(parts, 3)
    pl.semaphore_wait(barrier, len(NEAR))
    for dz in (1, 7):
        pl.semaphore_signal(ready1, inc=1, device_id=device(dz=dz), device_id_type=MESH)
    forward((0, 0), 0)
    for t in (1, 2):
        begin(("t", t), functools.partial(target_copy, t))
    forward((0, 0), 1)
    fetches[4].wait()
    acc[...] = jnp.zeros_like(acc)
    pl.semaphore_wait(ready1, 2)
    for dz in (2, 6):
        pl.semaphore_signal(ready2, inc=1, device_id=device(dz=dz), device_id_type=MESH)

    def block(sources, targets):
        cross = lax.dot_general(
            sources[0:DEEP], targets, (((0,), (0,)), ((), ())), preferred_element_type=F32
        )
        weights = jnp.exp(jnp.minimum(cross, 0.0)).astype(BF16)
        return jnp.dot(sources[DEEP:PACK], weights, preferred_element_type=F32)

    def pair_of(g):
        return jnp.concatenate([sbuf[g, 0], sbuf[g, 1]], axis=1)

    def quarter_of(t):
        return tbuf[t // 2, :, pl.ds(t % 2 * HALF if isinstance(t, int) else pl.multiple_of(t % 2 * HALF, HALF), HALF)]

    def target_here(t):
        target_copy(t).wait_recv()
        begin(("t", t + 2), functools.partial(target_relay, t))

    def far():
        pl.semaphore_wait(ready2, 2)
        for p in (0, 1):
            begin(("ring", (4, 0), p), functools.partial(ring, (0, 0), (4, 0), p, opposite))

    def at(step):
        def action():
            for pieces, part in ARRIVE.get(step, ()):
                for piece in pieces:
                    arrive(piece, part)
            for pair, part in CORE.get(step, ()):
                from_core(pair, part)
            for t in TARGET.get(step, ()):
                target_here(t)
            if step == FAR:
                far()
        return action

    def events(index, first, count):
        for n in range(count):
            if first + n in ARRIVE or first + n in CORE or first + n in TARGET or first + n == FAR:
                if isinstance(index, int):
                    if index == n:
                        at(first + n)()
                else:
                    pl.when(index == n)(at(first + n))

    def own_targets(part, carry):
        events(part, 0, 2)
        acc[0] += block(jnp.concatenate([sbuf[0, part], sbuf[1, part]], axis=1), tbuf[0, :, 0:HALF])
        return carry

    for n in range(2):
        own_targets(n, 0)

    def next_targets(m, carry):
        events(m, 2, 4)
        t = 1 + m // 2
        acc[t] += block(pair_of(m % 2), quarter_of(t))
        return carry

    for n in range(4):
        next_targets(n, 0)

    def middle(n, carry):
        events(n, 6, 10)

        def extra_block():
            for t in (1, 2):
                target_relay(t).wait_recv()
            both = jnp.concatenate([pair_of(0), pair_of(1)], axis=1)
            acc[3] += block(both, tbuf[1, :, HALF:])
            at(17)()

        if isinstance(n, int):
            if n == 1:
                extra_block()
        else:
            pl.when(n == 1)(extra_block)
        h = n % 2
        part = block(pair_of(2 + n // 2), tbuf[h])
        acc[2 * h] += part[:, 0:HALF]
        acc[2 * h + 1] += part[:, HALF:]
        return carry

    for n in range(10):
        middle(n, 0)
    at(16)()

    mine = x * 2 + yl

    def reduce_copy(t, dl):
        return copy(
            parting.at[t], reduced.at[mine], r_send.at[t, dl], r_recv.at[mine], device(dx=TARGET_X[t], dl=dl)
        )

    def leave(t):
        def action():
            for dl in (1, 0) if t else (1,):
                begin(("r", t, dl), functools.partial(reduce_copy, t, dl))
        return action

    def last(n, carry):
        t = 3 - n
        parting[t] = (acc[t] + block(pair_of(7), quarter_of(t))).astype(BF16)
        if isinstance(t, int):
            leave(t)()
        else:
            for s in (3, 2, 1, 0):
                pl.when(t == s)(leave(s))
        return carry

    part = block(pair_of(7), tbuf[1])
    for t in (3, 2):
        parting[t] = (acc[t] + part[:, (t - 2) * HALF:(t - 1) * HALF]).astype(BF16)
        leave(t)()
    for n in (2, 3):
        last(n, 0)
    reduced[mine] = parting[0]
    rhs = probes_ref[:, pl.ds(half_at, HALF)]
    diagonal = noise_ref[:, pl.ds(half_at, HALF)] * rhs
    norm = jnp.sum(rhs * rhs, axis=1, keepdims=True)
    for t in (3, 2, 1, 0):
        for dl in (1, 0) if t else (1,):
            other = ((x + TARGET_X[t]) % 4) * 2 + (yl + dl) % 2
            copy(
                parting.at[t], reduced.at[other], r_send.at[t, dl], r_recv.at[other], device(dx=TARGET_X[t], dl=dl)
            ).wait_recv()

    total = reduced[0].astype(F32)
    for n in range(1, 8):
        total = total + reduced[n].astype(F32)
    image = total + diagonal
    curve = jnp.sum(rhs * image, axis=1, keepdims=True)
    square = jnp.sum(image * image, axis=1, keepdims=True)

    lane = lax.broadcasted_iota(jnp.int32, (PROBES, 128), 1)
    probe = lax.broadcasted_iota(jnp.int32, (PROBES, 128), 0)
    spread = jnp.zeros((PROBES, 128), F32)
    for n, column in enumerate((norm, curve, square)):
        spread = jnp.where(lane == probe + PROBES * n, column, spread)
    here = pl.ds(loop * 2 + c, 1)
    sums[here, :] = jnp.sum(spread, axis=0, keepdims=True)
    for dx, dy, dz, dc in PEERS:
        copy(
            sums.at[here], sums.at[here], sum_send.at[0], sum_recv.at[0],
            device(dx=dx, dh=dy, dl=dy, dz=dz, dc=dc),
        ).start()
    span = pl.ds(half_at, HALF)
    image_ref[:, span] = image

    def image_copy(at):
        return copy(image_ref.at[:, at], image_ref.at[:, at], i_send.at[0], i_recv.at[0], sibling)

    begin("image", functools.partial(image_copy, span))
    image_copy(pl.ds(pl.multiple_of((1 - c) * HALF, HALF), HALF)).wait_recv()
    for make in started.values():
        make().wait_send()

    others = copy(
        sums.at[pl.ds(0, len(PEERS))], sums.at[pl.ds(0, len(PEERS))], sum_send.at[0], sum_recv.at[0], sibling
    )
    others.wait_recv()
    summed = jnp.sum(sums[...], axis=0, keepdims=True)

    def column(n):
        return jnp.sum(jnp.where(lane == probe + PROBES * n, summed, 0.0), axis=1, keepdims=True)

    norm, curve, square = column(0), column(1), column(2)
    alpha = norm / curve
    beta = jnp.maximum(alpha * alpha * square - norm, 0.0) / norm
    alpha_ref[...] = jnp.broadcast_to(alpha, (PROBES, SHARD))
    beta_ref[...] = jnp.broadcast_to(beta, (PROBES, SHARD))
    others.wait_send()


def local(descriptors, ard_scales, noise, probes):
    dma = pltpu.SemaphoreType.DMA
    shape = pltpu.VMEM((PROBES, SHARD), F32)
    alpha, image, beta = pl.pallas_call(
        kernel,
        out_shape=(shape, shape, shape),
        in_specs=[pl.BlockSpec(memory_space=pl.ANY)] * 4,
        out_specs=(pl.BlockSpec(memory_space=pltpu.VMEM),) * 3,
        scratch_shapes=[
            pltpu.VMEM((QUART, FEAT), BF16),
            pltpu.VMEM((HALF, FEAT), BF16),
            pltpu.VMEM((1, FEAT), F32),
            pltpu.VMEM((1, SHARD), F32),
            pltpu.VMEM((PROBES, SHARD), F32),
            pltpu.VMEM((8, 2, PACK, HALF), BF16),
            pltpu.VMEM((2, DEEP, 2 * HALF), BF16),
            pltpu.VMEM((4, PROBES, HALF), F32),
            pltpu.VMEM((4, PROBES, HALF), BF16),
            pltpu.VMEM((8, PROBES, HALF), BF16),
            pltpu.VMEM((128, 128), F32),
            dma((5,)),
            dma((8, 2, 2)), dma((8, 2, 2)), dma((5,)), dma((4, 2)), dma((1,)), dma((1,)),
            dma((8, 2, 2)), dma((8, 2, 2)), dma((5,)), dma((8,)), dma((1,)), dma((1,)),
            pltpu.SemaphoreType.REGULAR, pltpu.SemaphoreType.REGULAR,
        ],
        compiler_params=pltpu.CompilerParams(
            collective_id=0, has_side_effects=True, vmem_limit_bytes=56 << 20
        ),
        cost_estimate=pl.CostEstimate(flops=5_000_000_000, bytes_accessed=1_000_000, transcendentals=17_000_000),
        name="cg_step",
    )(descriptors, ard_scales.reshape(1, FEAT), noise.reshape(1, SHARD), probes)
    residual = probes - alpha * image
    return alpha * probes, residual, residual + beta * probes


def solution(mesh):
    return jax.shard_map(
        local,
        mesh=mesh,
        in_specs=(P("loop", None), P(), P("loop"), P(None, "loop")),
        out_specs=(P(None, "loop"), P(None, "loop"), P(None, "loop")),
        check_vma=False,
    )
```
